256 devices in a mesh: dp: 16 (over x, y_hi, core), seq: 16 (over y_lo, z).
Axes of the slice: x: 4, y: 4 (y_hi: 2, y_lo: 2; y = y_hi * 2 + y_lo), z: 8, core: 2. Of those that a mesh axis runs over, the one named last changes fastest.
Arguments:
- encoder_input: bfloat16 [16, 2048, 1536], P('dp'), may hold values from -6 to 6
- sublayer_norm_gain: float32 [1536], replicated, may hold values from 0.25 to 1.75
- sublayer_norm_bias: float32 [1536], replicated, may hold values from -3 to 3
- gate_up_weight: bfloat16 [2, 1536, 4096], P(None, None, 'seq'), may hold values from -0.15625 to 0.15625
- down_weight: bfloat16 [4096, 1536], P('seq'), may hold values from -0.09375 to 0.09375
- branch_layer_scale: float32 [1536], replicated, may hold values from 0.3 to 1
- closing_norm_gain: float32 [1536], replicated, may hold values from 0.25 to 1.75
- closing_norm_bias: float32 [1536], replicated, may hold values from -3 to 3
- diffusion_hidden: bfloat16 [16, 2048, 2048], P('dp', 'seq'), may hold values from -6 to 6
- projector_weight: bfloat16 [2048, 1536], P(('dp', 'seq')), may hold values from -0.125 to 0.125
Outputs:
- hidden_gradient: bfloat16 [16, 2048, 2048], P('dp', 'seq')
- grad_weight: float32 [2048, 1536], P(('dp', 'seq'))
The draws below stay inside these ranges and needn't reach their ends.
All inputs are finite; a program needn't handle non-finite values.
Results may differ from the reference program's by a relative error of at most 0.02.
Values may be sent and summed in bfloat16 or wider, within the bound.
A program may use at most 128 MiB of HBM per device.

```python
import math
import jax
import jax.numpy as jnp
from jax import lax

E = 1536
FF = 4096
PROJECTOR_WIDTH = 2048
PATCH_COUNT = 2048
IMAGE_COUNT = 16
N_SEQ = 16


def with_spikes(entries, own_key, source, target, parts, factor):
    owner, partner = [(jnp.arange(entries.shape[axis_at]) // (entries.shape[axis_at] // parts)).reshape([-1 if axis == axis_at else 1 for axis in range(entries.ndim)]) for axis_at in (source, target)]
    chosen = jax.random.permutation(own_key, parts)[partner]
    strong = (owner == chosen) | (owner == (partner + parts // 2) % parts)
    return jnp.where(strong, factor * entries, entries)


def levels(rng, dims, pieces, least, top_value):
    factor_of = 1.0
    for axis_at, blocks in pieces:
        steps = jax.random.uniform(jax.random.fold_in(jax.random.fold_in(rng, 6), axis_at), (blocks,), jnp.float32, least / len(pieces), top_value / len(pieces))
        factor_of = factor_of * jnp.repeat(jnp.exp(steps), dims[axis_at] // blocks).reshape((-1,) + (1,) * (len(dims) - 1 - axis_at))
    return factor_of


def normal_values(rng, shape, deviation, limit, split=(), kind=jnp.bfloat16):
    factor_of = levels(rng, shape, split, -0.22, 0.18) if split else 1.0
    result = jax.random.normal(rng, shape, jnp.float32) * deviation * factor_of
    return jnp.minimum(jnp.maximum(result, -limit), limit).astype(kind)


def heavy_noise(rng, dims, spread, most, cuts, heavy, dtype=jnp.bfloat16):
    result = spread * jax.random.normal(rng, dims, jnp.float32)
    if cuts:
        result = result * levels(rng, dims, cuts, -0.22, 0.18)
    return jnp.clip(with_spikes(result, jax.random.fold_in(rng, 3), *heavy), -most, most).astype(dtype)


def setup_inputs(seed: int = 0) -> dict:
    arg_keys = jax.random.split(jax.random.key(seed), 11)
    return {
        "encoder_input": normal_values(arg_keys[0], (IMAGE_COUNT, PATCH_COUNT, E), 1.0, 6.0, ((0, 16),)),
        "sublayer_norm_gain": jnp.clip(1.0 + 0.15 * jax.random.normal(arg_keys[1], (E,), jnp.float32), 0.25, 1.75),
        "sublayer_norm_bias": normal_values(arg_keys[2], (E,), 0.3, 3.0, (), jnp.float32),
        "gate_up_weight": normal_values(arg_keys[3], (2, E, FF), E ** -0.5, 0.15625, ((2, 16),)),
        "down_weight": normal_values(arg_keys[4], (FF, E), FF ** -0.5, 0.09375, ((0, 16),)),
        "branch_layer_scale": jnp.clip(jnp.exp(jax.random.uniform(arg_keys[5], (E,), jnp.float32, math.log(0.3), math.log(1.0))), 0.3, 1.0),
        "closing_norm_gain": jnp.clip(1.0 + 0.15 * jax.random.normal(arg_keys[6], (E,), jnp.float32), 0.25, 1.75),
        "closing_norm_bias": normal_values(arg_keys[7], (E,), 0.5, 3.0, (), jnp.float32),
        "diffusion_hidden": heavy_noise(arg_keys[8], (IMAGE_COUNT, PATCH_COUNT, PROJECTOR_WIDTH), 1.0, 6.0, ((0, 16), (1, 16)), (1, 2, 16, 2.0)),
        "projector_weight": normal_values(arg_keys[9], (PROJECTOR_WIDTH, E), PROJECTOR_WIDTH ** -0.5, 0.125, ((0, 256),)),
    }


def layer_norm(values, gain, shift):
    mean = lax.optimization_barrier(jnp.mean(values, axis=-1, keepdims=True))
    centered = values - mean
    var = lax.optimization_barrier(jnp.mean(centered * centered, axis=-1, keepdims=True))
    return centered / jnp.sqrt(var + 1e-06) * gain + shift

def encode_image(args):
    image, sublayer_norm_gain, sublayer_norm_bias, gate_up_weight, down_weight, branch_layer_scale, closing_norm_gain, closing_norm_bias = args
    inputs = image.astype(jnp.float32)
    normed = layer_norm(inputs, sublayer_norm_gain, sublayer_norm_bias).astype(jnp.bfloat16)
    gate = jnp.dot(normed, gate_up_weight[0], preferred_element_type=jnp.float32)
    up = jnp.dot(normed, gate_up_weight[1], preferred_element_type=jnp.float32)
    hidden = (jax.nn.silu(gate) * up).astype(jnp.bfloat16)
    groups = N_SEQ
    width = hidden.shape[1] // groups
    hidden_groups = hidden.reshape(hidden.shape[0], groups, width).transpose(1, 0, 2)
    down_groups = down_weight.reshape(groups, width, down_weight.shape[1])

    def add_group(grand_sum, pair):
        piece, rows = pair
        part = jnp.dot(piece, rows, preferred_element_type=jnp.float32).astype(jnp.bfloat16)
        return (grand_sum + part.astype(jnp.float32), None)
    branch, _ = lax.scan(add_group, jnp.zeros((hidden.shape[0], down_weight.shape[1]), jnp.float32), (hidden_groups, down_groups))
    return layer_norm(inputs + branch_layer_scale * branch, closing_norm_gain, closing_norm_bias)

def reference(encoder_input, sublayer_norm_gain, sublayer_norm_bias, gate_up_weight, down_weight, branch_layer_scale, closing_norm_gain, closing_norm_bias, diffusion_hidden, projector_weight):

    def one_image(image):
        return encode_image((image, sublayer_norm_gain, sublayer_norm_bias, gate_up_weight, down_weight, branch_layer_scale, closing_norm_gain, closing_norm_bias))
    target = lax.map(one_image, encoder_input)
    width = projector_weight.shape[1]
    grand_sum = diffusion_hidden.shape[0] * diffusion_hidden.shape[1]
    hidden_matrix = diffusion_hidden.reshape(grand_sum, diffusion_hidden.shape[2])
    flat_target = target.reshape(grand_sum, width)
    pred = jnp.dot(hidden_matrix, projector_weight, preferred_element_type=jnp.float32)
    pred_norm = jnp.sqrt(lax.optimization_barrier(jnp.sum(pred * pred, axis=-1, keepdims=True)) + 1e-06)
    target_norm = jnp.sqrt(lax.optimization_barrier(jnp.sum(flat_target * flat_target, axis=-1, keepdims=True)) + 1e-06)
    cosine = lax.optimization_barrier(jnp.sum(pred * flat_target, axis=-1, keepdims=True)) / (pred_norm * target_norm)
    grad_pred = -1.0 * width * (flat_target / (pred_norm * target_norm) - cosine * pred / (pred_norm * pred_norm))
    grad_pred = grad_pred.astype(jnp.bfloat16)
    hidden_gradient = lax.dot_general(grad_pred, projector_weight, (((1,), (1,)), ((), ())), preferred_element_type=jnp.float32)
    hidden_gradient = hidden_gradient.astype(jnp.bfloat16).reshape(diffusion_hidden.shape)
    grad_weight = lax.dot_general(hidden_matrix, grad_pred, (((0,), (0,)), ((), ())), preferred_element_type=jnp.float32)
    grad_weight = grad_weight / jnp.sqrt(jnp.float32(grand_sum))
    return (hidden_gradient, grad_weight)
```

```python
import functools

import jax
import jax.numpy as jnp
from jax import lax
from jax.experimental import pallas as pl
from jax.experimental.pallas import tpu as pltpu
from jax.sharding import PartitionSpec as P

F32 = jnp.float32
BF16 = jnp.bfloat16
EPS = 1e-06
TOKENS = 128
HALF_TOKENS = 1024
E = 1536
H = 768
Q = 384
WIDTH = 2048
HID = 256
SEMS = 128


def kernel(
    x_hbm, g1_ref, b1_ref, gu_hbm, dn_hbm, ls_ref, g2_ref, b2_ref, dh_hbm, pw_ref,
    hg_ref, gw_ref,
    xin, nrm, guo, dno, gux, dnx, hid, part, rz, w32, w, dh, dho, dht, pred,
    gp, gpall, ga, gb, ra, rb, sa, sb, ra2, rb2, s3, r3, res, fin,
    ssem, rsem, lsem,
):
    dp, seq = lax.axis_index("dp"), lax.axis_index("seq")
    x, yh, c = dp // 4, (dp // 2) % 2, dp % 2
    yl, z = seq // 8, seq % 8
    y = yh * 2 + yl

    def dev(xx, yy, zz, cc):
        return ((xx * 2 + yy // 2) * 2 + cc, (yy % 2) * 8 + zz)

    xp, xm, x2 = (x + 1) % 4, (x + 3) % 4, (x + 2) % 4
    yp, ym, y2 = (y + 1) % 4, (y + 3) % 4, (y + 2) % 4
    d_xp, d_xm = dev(xp, y, z, c), dev(xm, y, z, c)
    d_yp, d_ym = dev(x, yp, z, c), dev(x, ym, z, c)
    d_z = [None] + [dev(x, y, (z + k) % 8, c) for k in range(1, 8)]
    d_co = dev(x, y, z, 1 - c)

    barrier = pltpu.get_barrier_semaphore()
    peers = [d_xp, d_xm, d_yp, d_ym, d_co] + d_z[1:]
    for peer in peers:
        pl.semaphore_signal(barrier, inc=1, device_id=peer, device_id_type=pl.DeviceIdType.MESH)
    count = [0]
    sent = []

    def send(src, dst, device):
        k = count[0]
        count[0] += 1
        copy = pltpu.make_async_remote_copy(
            src_ref=src, dst_ref=dst, send_sem=ssem.at[k], recv_sem=rsem.at[k],
            device_id=device, device_id_type=pl.DeviceIdType.MESH,
        )
        copy.start()
        sent.append(copy)
        return copy

    def local(k, src, dst):
        copy = pltpu.make_async_copy(src, dst, lsem.at[k])
        copy.start()
        return copy

    c_x = local(0, x_hbm.at[pl.ds(pl.multiple_of(yl * HALF_TOKENS, HALF_TOKENS), HALF_TOKENS), :], xin)
    c_gu = local(1, gu_hbm, guo)
    c_dn = local(2, dn_hbm, dno)
    c_dh = local(3, dh_hbm, dh)
    w32[z] = pw_ref[...].astype(F32)
    pl.semaphore_wait(barrier, len(peers))

    def quarter(ref, side, core, size, lead):
        rows = pl.ds(pl.multiple_of((2 * side + core) * size, size), size)
        return ref.at[:, rows, :] if lead else ref.at[rows, :]

    f_gu = [send(quarter(gu_hbm, s, c, 384, True), quarter(gux, s, c, 384, True), d)
            for s, d in ((0, d_yp), (1, d_ym))]
    f_dn = [send(quarter(dn_hbm, s, c, 64, False), quarter(dnx, s, c, 64, False), d)
            for s, d in ((0, d_yp), (1, d_ym))]
    w_z = [send(w32.at[z], w32.at[z], d_z[k]) for k in (4, 3, 5, 2, 6, 1, 7)]
    c_dho = send(dh_hbm, dho, d_co)

    c_x.wait()
    gain1, bias1 = g1_ref[...].reshape(1, E), b1_ref[...].reshape(1, E)

    @pl.loop(0, HALF_TOKENS // 32)
    def _(i):
        rows = pl.ds(pl.multiple_of(i * 32, 32), 32)
        v = xin[rows, :].astype(F32)
        v = v - jnp.mean(v, axis=-1, keepdims=True)
        var = jnp.mean(v * v, axis=-1, keepdims=True)
        nrm[rows, :] = (v * lax.rsqrt(var + EPS) * gain1 + bias1).astype(BF16)

    def swish(values, weights):
        gate = jnp.dot(values, weights[0], preferred_element_type=F32)
        up = jnp.dot(values, weights[1], preferred_element_type=F32)
        return (gate * jax.nn.sigmoid(gate) * up).astype(BF16)

    c_gu.wait()

    @pl.loop(0, 4)
    def _(i):
        rows = pl.ds(pl.multiple_of(i * 256, 256), 256)
        hid[rows, :] = swish(nrm[rows, :], guo)

    for copy in w_z:
        copy.wait_recv()
    w[x, yh, c, yl] = w32[...].reshape(64, E).astype(BF16)
    col_a, col_b = pl.ds(0, H), pl.ds(H, H)
    a_l, a_r, b_l, b_r = (pl.ds(k * Q, Q) for k in range(4))

    def block(xx, yy, cols):
        return w.at[xx, yy // 2, c, yy % 2, :, cols]

    wa1 = [send(block(x, y, col_a), block(x, y, col_a), d) for d in (d_xp, d_xm)]
    wb1 = [send(block(x, y, col_b), block(x, y, col_b), d) for d in (d_yp, d_ym)]

    forwards = []
    for s, copy in ((0, f_gu[0]), (1, f_gu[1])):
        copy.wait_recv()
        piece = quarter(gux, s, c, 384, True)
        forwards.append(send(piece, piece, d_co))
    wa1[0].wait_recv()
    wa1r = [send(block(xm, y, a_l), block(xm, y, a_l), d_xp)]
    wa1[1].wait_recv()
    wa1r.append(send(block(xp, y, a_r), block(xp, y, a_r), d_xm))
    for s, copy in ((0, f_dn[0]), (1, f_dn[1])):
        copy.wait_recv()
        piece = quarter(dnx, s, c, 64, False)
        forwards.append(send(piece, piece, d_co))
    for copy in wa1r:
        copy.wait_recv()

    def column(yy, cols):
        return w.at[:, yy // 2, c, yy % 2, :, cols]

    def slab(xx, cols):
        return w.at[xx, :, c, :, :, cols]

    wa2 = [send(column(y, col_a), column(y, col_a), d) for d in (d_yp, d_ym)]
    c_dn.wait()
    for copy in forwards:
        copy.wait_recv()

    def ffn(ca, cb):
        ra_ = pl.ds(pl.multiple_of(ca * TOKENS, TOKENS), TOKENS)
        rb_ = pl.ds(pl.multiple_of(cb * TOKENS, TOKENS), TOKENS)
        values = jnp.concatenate([nrm[ra_, :], nrm[rb_, :]], axis=0)
        own = jnp.concatenate([hid[ra_, :], hid[rb_, :]], axis=0)
        other = swish(values, gux)
        for n in range(4):
            cols = pl.ds(n * Q, Q)
            out = jnp.dot(own, dno[:, cols], preferred_element_type=F32)
            out += jnp.dot(other, dnx[:, cols], preferred_element_type=F32)
            out = out.astype(BF16)
            cols = pl.ds((n % 2) * Q, Q)
            part[ca, n // 2, :, cols] = out[:TOKENS]
            part[cb, n // 2, :, cols] = out[TOKENS:]

    subs = [pl.ds(0, 64), pl.ds(64, 64)]
    ffn((z + 7) % 8, (z + 1) % 8)
    ring = []
    for sub in subs:
        ring.append([
            send(part.at[(z + 7) % 8, 0, sub, :], rz.at[0, 0, sub, :], d_z[1]),
            send(part.at[(z + 1) % 8, 1, sub, :], rz.at[1, 0, sub, :], d_z[7]),
        ])

    @pl.loop(1, 4)
    def _(j):
        ffn((z + 7 - j) % 8, (z + (j + 1) % 4) % 8)

    def ring_step(s):
        following = []
        for k, sub in enumerate(subs):
            pair = []
            for d in range(2):
                ring[k][d].wait_recv()
                chunk = (z + 6 - s) % 8 if d == 0 else (z + 2 + s) % 8
                total = rz[d, s, sub, :].astype(F32) + part[chunk, d, sub, :].astype(F32)
                rz[d, s, sub, :] = total.astype(BF16)
                pair.append(send(rz.at[d, s, sub, :], rz.at[d, s + 1, sub, :], d_z[1] if d == 0 else d_z[7]))
            following.append(pair)
        ring[:] = following

    ring_step(0)
    wb1[0].wait_recv()
    wb1r = [send(block(x, ym, b_l), block(x, ym, b_l), d_yp)]
    wb1[1].wait_recv()
    wb1r.append(send(block(x, yp, b_r), block(x, yp, b_r), d_ym))
    for copy in wb1r:
        copy.wait_recv()
    wb2 = [send(slab(x, col_b), slab(x, col_b), d) for d in (d_xp, d_xm)]
    ring_step(1)
    c_dh.wait()
    c_dho.wait_recv()

    @pl.loop(0, 4)
    def _(xx):
        for k in range(4):
            cols = pl.ds(pl.multiple_of(xx * 512 + k * 128, 128), 128)
            for t, ref in enumerate((dh, dho)):
                turned = ref[:, cols].T
                for low in range(2):
                    dht[xx, (k // 2) * 2 + low, pl.ds((k % 2) * 64, 64), pl.ds(t * 128, 128)] = (
                        turned[low * 64:(low + 1) * 64]
                    )

    ring_step(2)
    wa2[0].wait_recv()
    wa2r = [send(column(ym, a_l), column(ym, a_l), d_yp)]
    wa2[1].wait_recv()
    wa2r.append(send(column(yp, a_r), column(yp, a_r), d_ym))
    wb2[0].wait_recv()
    wb2r = [send(slab(xm, b_l), slab(xm, b_l), d_xp)]
    wb2[1].wait_recv()
    wb2r.append(send(slab(xp, b_r), slab(xp, b_r), d_xm))
    ring_step(3)
    ring_step(4)
    for copy in wa2r + wb2r:
        copy.wait_recv()
    w_co = send(w.at[:, :, c], w.at[:, :, c], d_co)
    ring_step(5)
    w_co.wait_recv()

    @pl.loop(0, 3)
    def _(n):
        cols = pl.ds(pl.multiple_of(n * 512, 512), 512)
        total = jnp.zeros((TOKENS, 512), F32)
        for k in range(4):
            total += jnp.dot(
                dh[:, pl.ds(k * 512, 512)], w[k, :, :, :, :, cols].reshape(512, 512),
                preferred_element_type=F32,
            )
        pred[:, cols] = total

    for k in range(2):
        for d in range(2):
            ring[k][d].wait_recv()
    scale, gain2, bias2 = (r[...].reshape(1, E) for r in (ls_ref, g2_ref, b2_ref))

    @pl.loop(0, TOKENS // 16)
    def _(i):
        rows = pl.ds(pl.multiple_of(i * 16, 16), 16)
        branch = jnp.concatenate(
            [part[z, d, rows, :].astype(F32) + rz[d, 6, rows, :].astype(F32) for d in range(2)], axis=1
        )
        own_rows = pl.ds(pl.multiple_of(z * TOKENS + i * 16, 16), 16)
        v = xin[own_rows, :].astype(F32) + scale * branch
        v = v - jnp.mean(v, axis=-1, keepdims=True)
        var = jnp.mean(v * v, axis=-1, keepdims=True)
        t = v * lax.rsqrt(var + EPS) * gain2 + bias2
        p = pred[rows, :]
        inv_p = lax.rsqrt(jnp.sum(p * p, axis=-1, keepdims=True) + EPS)
        inv_t = lax.rsqrt(jnp.sum(t * t, axis=-1, keepdims=True) + EPS)
        dot = jnp.sum(p * t, axis=-1, keepdims=True)
        lead = (-1.0 * E) * (inv_p * inv_t)
        grad = (lead * (t - (dot * inv_p * inv_p) * p)).astype(BF16)
        gp[0, rows, :] = grad[:, :H]
        gp[1, rows, :] = grad[:, H:]

    c_gp = send(gp.at[1 - c], gpall.at[pl.ds(128, 128), :], d_co)
    gpall[pl.ds(0, 128), :] = gp[c]
    c_gp.wait_recv()

    def grad_slab(xx):
        out = jnp.dot(dht[xx].reshape(512, 256), gpall[...], preferred_element_type=F32).astype(BF16)
        for half in range(2):
            ga[xx, half] = out[half * 256:(half + 1) * 256, :Q]
        for yy in range(4):
            gb[yy, xx // 2, pl.ds(pl.multiple_of((xx % 2) * 128, 128), 128), :] = (
                out[yy * 128:(yy + 1) * 128, Q:]
            )

    def first(g, r, two, plus, minus, dplus, dminus):
        return dict(
            l2=send(g.at[two, 0], r.at[0], dplus), r2=send(g.at[two, 1], r.at[3], dminus),
        )

    def second(o, g, r, plus, minus, dplus, dminus):
        o["ro"] = send(g.at[plus, 1], r.at[1], dplus)
        o["lo"] = send(g.at[minus, 0], r.at[4], dminus)

    def relay(o, g, r, plus, minus, dplus, dminus):
        o["l2"].wait_recv()
        r[0] = (r[0].astype(F32) + g[plus, 0].astype(F32)).astype(BF16)
        o["ls"] = send(r.at[0], r.at[2], dplus)
        o["r2"].wait_recv()
        r[3] = (r[3].astype(F32) + g[minus, 1].astype(F32)).astype(BF16)
        o["rs"] = send(r.at[3], r.at[5], dminus)

    def total(o, g, r, me):
        for name in ("ro", "lo", "ls", "rs"):
            o[name].wait_recv()
        left = g[me, 0].astype(F32) + r[2].astype(F32) + r[4].astype(F32)
        right = g[me, 1].astype(F32) + r[1].astype(F32) + r[5].astype(F32)
        return left, right

    on_x, on_y = (xp, xm, d_xp, d_xm), (yp, ym, d_yp, d_ym)
    grad_slab(x2)
    oa = first(ga, ra, x2, *on_x)
    grad_slab(xp)
    grad_slab(xm)
    second(oa, ga, ra, *on_x)
    grad_slab(x)
    ob = first(gb, rb, y2, *on_y)
    second(ob, gb, rb, *on_y)

    def hidden_gradient(k):
        rows = w.at[k]
        out = jnp.zeros((TOKENS, 512), F32)
        for d in range(2):
            out += lax.dot_general(
                gp[d], rows[:, :, :, :, pl.ds(d * H, H)].reshape(512, H),
                (((1,), (1,)), ((), ())), preferred_element_type=F32,
            )
        hg_ref[0, :, pl.ds(pl.multiple_of(k * 512, 512), 512)] = out.astype(BF16)

    @pl.loop(0, 2)
    def _(k):
        hidden_gradient(k)

    relay(oa, ga, ra, *on_x)
    relay(ob, gb, rb, *on_y)

    @pl.loop(2, 4)
    def _(k):
        hidden_gradient(k)

    left, right = total(oa, ga, ra, x)
    for k, half in enumerate((left, right)):
        half = half.astype(BF16)
        for q in range(4):
            sa[2 * k + q // 2, q % 2] = half[q * 64:(q + 1) * 64]
    oa2 = first(sa, ra2, y2, *on_y)
    second(oa2, sa, ra2, *on_y)
    left, right = total(ob, gb, rb, y)
    for k, half in enumerate((left, right)):
        half = half.astype(BF16)
        for q in range(4):
            sb[2 * k + q // 2, q % 2] = half[q * 64:(q + 1) * 64]
    ob2 = first(sb, rb2, x2, *on_x)
    second(ob2, sb, rb2, *on_x)
    relay(oa2, sa, ra2, *on_y)
    relay(ob2, sb, rb2, *on_x)
    for k, (o, s, r, me) in enumerate(((oa2, sa, ra2, y), (ob2, sb, rb2, x))):
        left, right = total(o, s, r, me)
        both = jnp.concatenate([left.reshape(8, 8, Q), right.reshape(8, 8, Q)], axis=1)
        s3[:, :, pl.ds(k * Q, Q)] = both.astype(BF16)
    last = [send(s3.at[(z + k) % 8], r3.at[z], d_z[k]) for k in (4, 3, 5, 2, 6, 1, 7)]
    r3[z] = s3[z]
    for copy in last:
        copy.wait_recv()
    tot = jnp.sum(r3[...].astype(F32), axis=0) * (1.0 / (16 * 2048) ** 0.5)
    res[0] = tot[:8]
    res[1] = tot[8:]
    c_fin = send(res.at[1 - c], fin, d_co)
    gw_ref[:, pl.ds(pl.multiple_of(c * H, H), H)] = res[c]
    for copy in sent[:-1]:
        copy.wait_send()
    c_fin.wait_recv()
    gw_ref[:, pl.ds(pl.multiple_of((1 - c) * H, H), H)] = fin[...]
    c_fin.wait_send()


def on_device(
    encoder_input, sublayer_norm_gain, sublayer_norm_bias, gate_up_weight, down_weight,
    branch_layer_scale, closing_norm_gain, closing_norm_bias, diffusion_hidden, projector_weight,
):
    hbm = pl.BlockSpec(memory_space=pl.ANY)
    vmem = pl.BlockSpec(memory_space=pltpu.VMEM)
    return pl.pallas_call(
        kernel,
        out_shape=(
            jax.ShapeDtypeStruct((1, TOKENS, WIDTH), BF16),
            jax.ShapeDtypeStruct((8, E), F32),
        ),
        in_specs=[hbm, vmem, vmem, hbm, hbm, vmem, vmem, vmem, hbm, vmem],
        out_specs=(vmem, vmem),
        scratch_shapes=[
            pltpu.VMEM((HALF_TOKENS, E), BF16),
            pltpu.VMEM((HALF_TOKENS, E), BF16),
            pltpu.VMEM((2, E, HID), BF16),
            pltpu.VMEM((HID, E), BF16),
            pltpu.VMEM((2, E, HID), BF16),
            pltpu.VMEM((HID, E), BF16),
            pltpu.VMEM((HALF_TOKENS, HID), BF16),
            pltpu.VMEM((8, 2, TOKENS, H), BF16),
            pltpu.VMEM((2, 7, TOKENS, H), BF16),
            pltpu.VMEM((8, 8, E), F32),
            pltpu.VMEM((4, 2, 2, 2, 64, E), BF16),
            pltpu.VMEM((TOKENS, WIDTH), BF16),
            pltpu.VMEM((TOKENS, WIDTH), BF16),
            pltpu.VMEM((4, 4, 128, 256), BF16),
            pltpu.VMEM((TOKENS, E), F32),
            pltpu.VMEM((2, TOKENS, H), BF16),
            pltpu.VMEM((256, H), BF16),
            pltpu.VMEM((4, 2, 256, Q), BF16),
            pltpu.VMEM((4, 2, 256, Q), BF16),
            pltpu.VMEM((6, 256, Q), BF16),
            pltpu.VMEM((6, 256, Q), BF16),
            pltpu.VMEM((4, 2, 64, Q), BF16),
            pltpu.VMEM((4, 2, 64, Q), BF16),
            pltpu.VMEM((6, 64, Q), BF16),
            pltpu.VMEM((6, 64, Q), BF16),
            pltpu.VMEM((8, 16, H), BF16),
            pltpu.VMEM((8, 16, H), BF16),
            pltpu.VMEM((2, 8, H), F32),
            pltpu.VMEM((8, H), F32),
            pltpu.SemaphoreType.DMA((SEMS,)),
            pltpu.SemaphoreType.DMA((SEMS,)),
            pltpu.SemaphoreType.DMA((4,)),
        ],
        compiler_params=pltpu.CompilerParams(
            collective_id=0, has_side_effects=True, vmem_limit_bytes=56 * 1024 * 1024
        ),
    )(
        encoder_input[0], sublayer_norm_gain, sublayer_norm_bias, gate_up_weight, down_weight,
        branch_layer_scale, closing_norm_gain, closing_norm_bias, diffusion_hidden[0], projector_weight,
    )


def solution(mesh):
    in_specs = (
        P("dp", None, None), P(), P(), P(None, None, "seq"), P("seq", None), P(), P(), P(),
        P("dp", "seq", None), P(("dp", "seq"), None),
    )
    out_specs = (P("dp", "seq", None), P(("dp", "seq"), None))
    return jax.shard_map(
        on_device, mesh=mesh, in_specs=in_specs, out_specs=out_specs, check_vma=False
    )
```

```python
import functools

import jax
import jax.numpy as jnp
from jax import lax
from jax.experimental import pallas as pl
from jax.experimental.pallas import tpu as pltpu
from jax.sharding import PartitionSpec as P

F32 = jnp.float32
BF16 = jnp.bfloat16
EPS = 1e-06
TOKENS = 128
EARLY = 32
LATE = 96
E = 1536
H = 768
Q = 384
WIDTH = 2048
HID = 256
SEMS = 160


def kernel(
    x_hbm, g1_ref, b1_ref, gu_hbm, dn_hbm, ls_ref, g2_ref, b2_ref, dh_hbm, pw_ref,
    hg_ref, gw_ref,
    xs, xl, ns, nl, guo, dno, gux, dnx, hl, ep, re, es, ex, lp, rl, wu, w, dh, dho, dht, pred,
    gp, gpall, ga, gb, ra, rb, sa, sb, ra2, rb2, s3, r3, res, fin,
    ssem, rsem, lsem,
):
    dp, seq = lax.axis_index("dp"), lax.axis_index("seq")
    x, yh, c = dp // 4, (dp // 2) % 2, dp % 2
    yl, z = seq // 8, seq % 8
    y = yh * 2 + yl

    def dev(xx, yy, zz, cc):
        return ((xx * 2 + yy // 2) * 2 + cc, (yy % 2) * 8 + zz)

    xp, xm, x2 = (x + 1) % 4, (x + 3) % 4, (x + 2) % 4
    yp, ym, y2 = (y + 1) % 4, (y + 3) % 4, (y + 2) % 4
    d_xp, d_xm = dev(xp, y, z, c), dev(xm, y, z, c)
    d_yp, d_ym = dev(x, yp, z, c), dev(x, ym, z, c)
    d_z = [None] + [dev(x, y, (z + k) % 8, c) for k in range(1, 8)]
    d_co = dev(x, y, z, 1 - c)
    d_pair = dev(x, yh * 2 + 1 - yl, z, c)

    barrier = pltpu.get_barrier_semaphore()
    peers = [d_xp, d_xm, d_yp, d_ym, d_co] + d_z[1:]
    for peer in peers:
        pl.semaphore_signal(barrier, inc=1, device_id=peer, device_id_type=pl.DeviceIdType.MESH)
    count = [0]
    sent = []

    def send(src, dst, device):
        k = count[0]
        count[0] += 1
        copy = pltpu.make_async_remote_copy(
            src_ref=src, dst_ref=dst, send_sem=ssem.at[k], recv_sem=rsem.at[k],
            device_id=device, device_id_type=pl.DeviceIdType.MESH,
        )
        copy.start()
        sent.append(copy)
        return copy

    def local(k, src, dst):
        copy = pltpu.make_async_copy(src, dst, lsem.at[k])
        copy.start()
        return copy

    c_xs = local(0, x_hbm.at[:, pl.ds(0, EARLY), :], xs)
    c_gu = local(1, gu_hbm, guo)
    c_dn = local(2, dn_hbm, dno)
    c_xl = local(3, x_hbm.at[pl.ds(yl * 8, 8), pl.ds(EARLY, LATE), :], xl)
    c_dh = local(4, dh_hbm, dh)
    rows_w = pw_ref[...].astype(F32)
    wu[z] = jnp.concatenate([rows_w[:, :H], rows_w[:, H:]], axis=0).astype(BF16)
    gain1, bias1 = g1_ref[...].reshape(1, E), b1_ref[...].reshape(1, E)

    def norm(v):
        v = v.astype(F32)
        v = v - jnp.mean(v, axis=-1, keepdims=True)
        var = jnp.mean(v * v, axis=-1, keepdims=True)
        return (v * lax.rsqrt(var + EPS) * gain1 + bias1).astype(BF16)

    def swish(values, weights):
        gate = jnp.dot(values, weights[0], preferred_element_type=F32)
        up = jnp.dot(values, weights[1], preferred_element_type=F32)
        return (gate * jax.nn.sigmoid(gate) * up).astype(BF16)

    def chunks(j):
        return (z + 7 - j) % 8, (z + (j + 1) % 4) % 8

    def norm_early(j):
        for chunk in chunks(j):
            ns[chunk, pl.ds(0, EARLY), :] = norm(xs[yl * 8 + chunk])
            ns[chunk, pl.ds(EARLY, EARLY), :] = norm(xs[(1 - yl) * 8 + chunk])

    c_xs.wait()
    norm_early(0)
    pl.semaphore_wait(barrier, len(peers))

    def quarter(ref, side, core, size, lead):
        rows = pl.ds(pl.multiple_of((2 * side + core) * size, size), size)
        return ref.at[:, rows, :] if lead else ref.at[rows, :]

    f_gu = [send(quarter(gu_hbm, s, c, 384, True), quarter(gux, s, c, 384, True), d)
            for s, d in ((0, d_yp), (1, d_ym))]
    f_dn = [send(quarter(dn_hbm, s, c, 64, False), quarter(dnx, s, c, 64, False), d)
            for s, d in ((0, d_yp), (1, d_ym))]

    def unit(k):
        return wu.at[(z + k) % 8]

    wz = [send(unit(0), unit(0), d_z[1]), send(unit(0), unit(0), d_z[7])]
    c_dho = send(dh_hbm, dho, d_co)

    def ffn_early(j):
        ca, cb = chunks(j)
        hidden = swish(jnp.concatenate([ns[ca], ns[cb]], axis=0), guo)
        for n in range(4):
            out = jnp.dot(hidden, dno[:, pl.ds(n * Q, Q)], preferred_element_type=F32).astype(BF16)
            cols = pl.ds((n % 2) * Q, Q)
            ep[ca, n // 2, :, cols] = out[:64]
            ep[cb, n // 2, :, cols] = out[64:]

    def ring_start(p, r, subs):
        return [[
            send(p.at[(z + 7) % 8, 0, sub, :], r.at[0, 0, sub, :], d_z[1]),
            send(p.at[(z + 1) % 8, 1, sub, :], r.at[1, 0, sub, :], d_z[7]),
        ] for sub in subs]

    def ring_step(s, ring, p, r, subs):
        following = []
        for k, sub in enumerate(subs):
            pair = []
            for d in range(2):
                ring[k][d].wait_recv()
                chunk = (z + 6 - s) % 8 if d == 0 else (z + 2 + s) % 8
                both = r[d, s, sub, :].astype(F32) + p[chunk, d, sub, :].astype(F32)
                r[d, s, sub, :] = both.astype(BF16)
                pair.append(send(r.at[d, s, sub, :], r.at[d, s + 1, sub, :], d_z[1] if d == 0 else d_z[7]))
            following.append(pair)
        ring[:] = following

    e_subs = [pl.ds(0, EARLY), pl.ds(EARLY, EARLY)]
    l_subs = [pl.ds(0, 48), pl.ds(48, 48)]
    c_gu.wait()
    c_dn.wait()
    ffn_early(0)
    e_ring = ring_start(ep, re, e_subs)
    norm_early(1)
    ffn_early(1)
    for copy in wz:
        copy.wait_recv()
    wz = [send(unit(7), unit(7), d_z[1]), send(unit(1), unit(1), d_z[7])]
    ring_step(0, e_ring, ep, re, e_subs)
    norm_early(2)
    ffn_early(2)
    for copy in wz:
        copy.wait_recv()
    wz = [send(unit(6), unit(6), d_z[1]), send(unit(2), unit(2), d_z[7])]
    ring_step(1, e_ring, ep, re, e_subs)
    norm_early(3)
    ffn_early(3)
    for copy in wz:
        copy.wait_recv()
    wz = [send(unit(5), unit(5), d_z[1])]
    ring_step(2, e_ring, ep, re, e_subs)

    def prepare_late(j):
        for chunk in chunks(j):
            @pl.loop(0, LATE // 32)
            def _(i):
                rows = pl.ds(pl.multiple_of(i * 32, 32), 32)
                nl[chunk, rows, :] = norm(xl[chunk, rows, :])

        ca, cb = chunks(j)
        hidden = swish(jnp.concatenate([nl[ca], nl[cb]], axis=0), guo)
        hl[ca] = hidden[:LATE]
        hl[cb] = hidden[LATE:]

    c_xl.wait()
    prepare_late(0)
    wz[0].wait_recv()
    units = wu[...].astype(F32)
    w[x, yh, c, yl, :, pl.ds(0, H)] = units[:, :8].reshape(64, H).astype(BF16)
    w[x, yh, c, yl, :, pl.ds(H, H)] = units[:, 8:].reshape(64, H).astype(BF16)
    col_a, col_b = pl.ds(0, H), pl.ds(H, H)
    a_l, a_r, b_l, b_r = (pl.ds(k * Q, Q) for k in range(4))

    def block(xx, yy, cols):
        return w.at[xx, yy // 2, c, yy % 2, :, cols]

    def column(yy, cols):
        return w.at[:, yy // 2, c, yy % 2, :, cols]

    def slab(xx, cols):
        return w.at[xx, :, c, :, :, cols]

    def core_half(cols):
        return w.at[:, :, c, :, :, cols]

    def same(piece, device):
        return send(piece, piece, device)

    wa1 = [same(block(x, y, col_a), d) for d in (d_xp, d_xm)]
    wb1 = [same(block(x, y, col_b), d) for d in (d_yp, d_ym)]
    ring_step(3, e_ring, ep, re, e_subs)
    prepare_late(1)
    wa1[0].wait_recv()
    wa1r = [same(block(xm, y, a_l), d_xp)]
    wa1[1].wait_recv()
    wa1r.append(same(block(xp, y, a_r), d_xm))
    forwards = []
    for s, copy in ((0, f_gu[0]), (1, f_gu[1])):
        copy.wait_recv()
        forwards.append(same(quarter(gux, s, c, 384, True), d_co))
    ring_step(4, e_ring, ep, re, e_subs)
    prepare_late(2)
    for copy in wa1r:
        copy.wait_recv()
    wa2 = [same(column(y, col_a), d) for d in (d_yp, d_ym)]
    ring_step(5, e_ring, ep, re, e_subs)
    prepare_late(3)
    for s, copy in ((0, f_dn[0]), (1, f_dn[1])):
        copy.wait_recv()
        forwards.append(same(quarter(dnx, s, c, 64, False), d_co))
    for copy in forwards:
        copy.wait_recv()

    def ffn_late(j):
        ca, cb = chunks(j)
        other = swish(jnp.concatenate([nl[ca], nl[cb]], axis=0), gux)
        own = jnp.concatenate([hl[ca], hl[cb]], axis=0)
        for n in range(4):
            cols = pl.ds(n * Q, Q)
            out = jnp.dot(own, dno[:, cols], preferred_element_type=F32)
            out += jnp.dot(other, dnx[:, cols], preferred_element_type=F32)
            out = out.astype(BF16)
            cols = pl.ds((n % 2) * Q, Q)
            lp[ca, n // 2, :, cols] = out[:LATE]
            lp[cb, n // 2, :, cols] = out[LATE:]

    ffn_late(0)
    l_ring = ring_start(lp, rl, l_subs)
    for pair in e_ring:
        for copy in pair:
            copy.wait_recv()
    for d in range(2):
        es[d] = (re[d, 6, e_subs[1], :].astype(F32) + ep[z, d, e_subs[1], :].astype(F32)).astype(BF16)
    c_ex = send(es, ex, d_pair)
    wb1[0].wait_recv()
    wb1r = [same(block(x, ym, b_l), d_yp)]
    wb1[1].wait_recv()
    wb1r.append(same(block(x, yp, b_r), d_ym))

    @pl.loop(1, 3)
    def _(j):
        ffn_late(j)

    for copy in wb1r:
        copy.wait_recv()
    wb2 = [same(slab(x, col_b), d) for d in (d_xp, d_xm)]
    ffn_late(3)
    ring_step(0, l_ring, lp, rl, l_subs)
    c_dh.wait()
    c_dho.wait_recv()

    @pl.loop(0, 4)
    def _(xx):
        for k in range(4):
            cols = pl.ds(pl.multiple_of(xx * 512 + k * 128, 128), 128)
            for t, ref in enumerate((dh, dho)):
                turned = ref[:, cols].T
                for low in range(2):
                    dht[xx, (k // 2) * 2 + low, pl.ds((k % 2) * 64, 64), pl.ds(t * 128, 128)] = (
                        turned[low * 64:(low + 1) * 64]
                    )

    ring_step(1, l_ring, lp, rl, l_subs)
    wa2[0].wait_recv()
    wa2r = [same(column(ym, a_l), d_yp)]
    wa2[1].wait_recv()
    wa2r.append(same(column(yp, a_r), d_ym))
    ring_step(2, l_ring, lp, rl, l_subs)
    wb2[0].wait_recv()
    wb2r = [same(slab(xm, b_l), d_xp)]
    wb2[1].wait_recv()
    wb2r.append(same(slab(xp, b_r), d_xm))
    ring_step(3, l_ring, lp, rl, l_subs)
    for copy in wa2r:
        copy.wait_recv()
    w_co = [same(core_half(col_a), d_co)]
    ring_step(4, l_ring, lp, rl, l_subs)
    for copy in wb2r:
        copy.wait_recv()
    w_co.append(same(core_half(col_b), d_co))
    ring_step(5, l_ring, lp, rl, l_subs)
    for copy in w_co:
        copy.wait_recv()

    @pl.loop(0, 3)
    def _(n):
        cols = pl.ds(pl.multiple_of(n * 512, 512), 512)
        acc = jnp.zeros((TOKENS, 512), F32)
        for k in range(4):
            acc += jnp.dot(
                dh[:, pl.ds(k * 512, 512)], w[k, :, :, :, :, cols].reshape(512, 512),
                preferred_element_type=F32,
            )
        pred[:, cols] = acc

    scale, gain2, bias2 = (r[...].reshape(1, E) for r in (ls_ref, g2_ref, b2_ref))

    def loss_gradient(own, branch, rows):
        v = own.astype(F32) + scale * jnp.concatenate(branch, axis=1)
        v = v - jnp.mean(v, axis=-1, keepdims=True)
        var = jnp.mean(v * v, axis=-1, keepdims=True)
        t = v * lax.rsqrt(var + EPS) * gain2 + bias2
        p = pred[rows, :]
        inv_p = lax.rsqrt(jnp.sum(p * p, axis=-1, keepdims=True) + EPS)
        inv_t = lax.rsqrt(jnp.sum(t * t, axis=-1, keepdims=True) + EPS)
        dot = jnp.sum(p * t, axis=-1, keepdims=True)
        lead = (-1.0 * E) * (inv_p * inv_t)
        grad = (lead * (t - (dot * inv_p * inv_p) * p)).astype(BF16)
        gp[0, rows, :] = grad[:, :H]
        gp[1, rows, :] = grad[:, H:]

    def swap_gradient(start, size):
        gpall[pl.ds(start, size), :] = gp[c, pl.ds(start, size), :]
        return send(gp.at[1 - c, pl.ds(start, size), :], gpall.at[pl.ds(128 + start, size), :], d_co)

    c_ex.wait_recv()

    @pl.loop(0, EARLY // 16)
    def _(i):
        rows = pl.ds(pl.multiple_of(i * 16, 16), 16)
        branch = [
            ep[z, d, rows, :].astype(F32) + re[d, 6, rows, :].astype(F32) + ex[d, rows, :].astype(F32)
            for d in range(2)
        ]
        loss_gradient(xs[yl * 8 + z, rows, :], branch, rows)

    c_gp = [swap_gradient(0, EARLY)]
    for k in range(2):
        for d in range(2):
            l_ring[k][d].wait_recv()

        @pl.loop(3 * k, 3 * k + 3)
        def _(i):
            rows = pl.ds(pl.multiple_of(i * 16, 16), 16)
            branch = [lp[z, d, rows, :].astype(F32) + rl[d, 6, rows, :].astype(F32) for d in range(2)]
            loss_gradient(xl[z, rows, :], branch, pl.ds(pl.multiple_of(EARLY + i * 16, 16), 16))

        c_gp.append(swap_gradient(EARLY + 48 * k, 48))
    for copy in c_gp:
        copy.wait_recv()

    def grad_slab(xx):
        out = jnp.dot(dht[xx].reshape(512, 256), gpall[...], preferred_element_type=F32).astype(BF16)
        for half in range(2):
            ga[xx, half] = out[half * 256:(half + 1) * 256, :Q]
        for yy in range(4):
            gb[yy, xx // 2, pl.ds(pl.multiple_of((xx % 2) * 128, 128), 128), :] = (
                out[yy * 128:(yy + 1) * 128, Q:]
            )

    def first(g, r, two, plus, minus, dplus, dminus):
        return dict(
            l2=send(g.at[two, 0], r.at[0], dplus), r2=send(g.at[two, 1], r.at[3], dminus),
        )

    def second(o, g, r, plus, minus, dplus, dminus):
        o["ro"] = send(g.at[plus, 1], r.at[1], dplus)
        o["lo"] = send(g.at[minus, 0], r.at[4], dminus)

    def relay(o, g, r, plus, minus, dplus, dminus):
        o["l2"].wait_recv()
        r[0] = (r[0].astype(F32) + g[plus, 0].astype(F32)).astype(BF16)
        o["ls"] = send(r.at[0], r.at[2], dplus)
        o["r2"].wait_recv()
        r[3] = (r[3].astype(F32) + g[minus, 1].astype(F32)).astype(BF16)
        o["rs"] = send(r.at[3], r.at[5], dminus)

    def total(o, g, r, me):
        for name in ("ro", "lo", "ls", "rs"):
            o[name].wait_recv()
        left = g[me, 0].astype(F32) + r[2].astype(F32) + r[4].astype(F32)
        right = g[me, 1].astype(F32) + r[1].astype(F32) + r[5].astype(F32)
        return left, right

    on_x, on_y = (xp, xm, d_xp, d_xm), (yp, ym, d_yp, d_ym)
    grad_slab(x2)
    oa = first(ga, ra, x2, *on_x)
    grad_slab(xp)
    grad_slab(xm)
    second(oa, ga, ra, *on_x)
    grad_slab(x)
    ob = first(gb, rb, y2, *on_y)
    second(ob, gb, rb, *on_y)

    def hidden_gradient(k):
        rows = w.at[k]
        out = jnp.zeros((TOKENS, 512), F32)
        for d in range(2):
            out += lax.dot_general(
                gp[d], rows[:, :, :, :, pl.ds(d * H, H)].reshape(512, H),
                (((1,), (1,)), ((), ())), preferred_element_type=F32,
            )
        hg_ref[0, :, pl.ds(pl.multiple_of(k * 512, 512), 512)] = out.astype(BF16)

    @pl.loop(0, 2)
    def _(k):
        hidden_gradient(k)

    relay(oa, ga, ra, *on_x)
    relay(ob, gb, rb, *on_y)

    @pl.loop(2, 4)
    def _(k):
        hidden_gradient(k)

    left, right = total(oa, ga, ra, x)
    for k, half in enumerate((left, right)):
        half = half.astype(BF16)
        for q in range(4):
            sa[2 * k + q // 2, q % 2] = half[q * 64:(q + 1) * 64]
    oa2 = first(sa, ra2, y2, *on_y)
    second(oa2, sa, ra2, *on_y)
    left, right = total(ob, gb, rb, y)
    for k, half in enumerate((left, right)):
        half = half.astype(BF16)
        for q in range(4):
            sb[2 * k + q // 2, q % 2] = half[q * 64:(q + 1) * 64]
    ob2 = first(sb, rb2, x2, *on_x)
    second(ob2, sb, rb2, *on_x)
    relay(oa2, sa, ra2, *on_y)
    relay(ob2, sb, rb2, *on_x)
    for k, (o, s, r, me) in enumerate(((oa2, sa, ra2, y), (ob2, sb, rb2, x))):
        left, right = total(o, s, r, me)
        both = jnp.concatenate([left.reshape(8, 8, Q), right.reshape(8, 8, Q)], axis=1)
        s3[:, :, pl.ds(k * Q, Q)] = both.astype(BF16)
    last = [send(s3.at[(z + k) % 8], r3.at[z], d_z[k]) for k in (4, 3, 5, 2, 6, 1, 7)]
    r3[z] = s3[z]
    for copy in last:
        copy.wait_recv()
    tot = jnp.sum(r3[...].astype(F32), axis=0) * (1.0 / (16 * 2048) ** 0.5)
    res[0] = tot[:8]
    res[1] = tot[8:]
    c_fin = send(res.at[1 - c], fin, d_co)
    gw_ref[:, pl.ds(pl.multiple_of(c * H, H), H)] = res[c]
    for copy in sent[:-1]:
        copy.wait_send()
    c_fin.wait_recv()
    gw_ref[:, pl.ds(pl.multiple_of((1 - c) * H, H), H)] = fin[...]
    c_fin.wait_send()


def on_device(
    encoder_input, sublayer_norm_gain, sublayer_norm_bias, gate_up_weight, down_weight,
    branch_layer_scale, closing_norm_gain, closing_norm_bias, diffusion_hidden, projector_weight,
):
    hbm = pl.BlockSpec(memory_space=pl.ANY)
    vmem = pl.BlockSpec(memory_space=pltpu.VMEM)
    return pl.pallas_call(
        kernel,
        out_shape=(
            jax.ShapeDtypeStruct((1, TOKENS, WIDTH), BF16),
            jax.ShapeDtypeStruct((8, E), F32),
        ),
        in_specs=[hbm, vmem, vmem, hbm, hbm, vmem, vmem, vmem, hbm, vmem],
        out_specs=(vmem, vmem),
        scratch_shapes=[
            pltpu.VMEM((16, EARLY, E), BF16),
            pltpu.VMEM((8, LATE, E), BF16),
            pltpu.VMEM((8, 2 * EARLY, E), BF16),
            pltpu.VMEM((8, LATE, E), BF16),
            pltpu.VMEM((2, E, HID), BF16),
            pltpu.VMEM((HID, E), BF16),
            pltpu.VMEM((2, E, HID), BF16),
            pltpu.VMEM((HID, E), BF16),
            pltpu.VMEM((8, LATE, HID), BF16),
            pltpu.VMEM((8, 2, 2 * EARLY, H), BF16),
            pltpu.VMEM((2, 7, 2 * EARLY, H), BF16),
            pltpu.VMEM((2, EARLY, H), BF16),
            pltpu.VMEM((2, EARLY, H), BF16),
            pltpu.VMEM((8, 2, LATE, H), BF16),
            pltpu.VMEM((2, 7, LATE, H), BF16),
            pltpu.VMEM((8, 16, H), BF16),
            pltpu.VMEM((4, 2, 2, 2, 64, E), BF16),
            pltpu.VMEM((TOKENS, WIDTH), BF16),
            pltpu.VMEM((TOKENS, WIDTH), BF16),
            pltpu.VMEM((4, 4, 128, 256), BF16),
            pltpu.VMEM((TOKENS, E), F32),
            pltpu.VMEM((2, TOKENS, H), BF16),
            pltpu.VMEM((256, H), BF16),
            pltpu.VMEM((4, 2, 256, Q), BF16),
            pltpu.VMEM((4, 2, 256, Q), BF16),
            pltpu.VMEM((6, 256, Q), BF16),
            pltpu.VMEM((6, 256, Q), BF16),
            pltpu.VMEM((4, 2, 64, Q), BF16),
            pltpu.VMEM((4, 2, 64, Q), BF16),
            pltpu.VMEM((6, 64, Q), BF16),
            pltpu.VMEM((6, 64, Q), BF16),
            pltpu.VMEM((8, 16, H), BF16),
            pltpu.VMEM((8, 16, H), BF16),
            pltpu.VMEM((2, 8, H), F32),
            pltpu.VMEM((8, H), F32),
            pltpu.SemaphoreType.DMA((SEMS,)),
            pltpu.SemaphoreType.DMA((SEMS,)),
            pltpu.SemaphoreType.DMA((5,)),
        ],
        compiler_params=pltpu.CompilerParams(
            collective_id=0, has_side_effects=True, vmem_limit_bytes=56 * 1024 * 1024
        ),
    )(
        encoder_input[0].reshape(16, TOKENS, E), sublayer_norm_gain, sublayer_norm_bias, gate_up_weight, down_weight,
        branch_layer_scale, closing_norm_gain, closing_norm_bias, diffusion_hidden[0], projector_weight,
    )


def solution(mesh):
    in_specs = (
        P("dp", None, None), P(), P(), P(None, None, "seq"), P("seq", None), P(), P(), P(),
        P("dp", "seq", None), P(("dp", "seq"), None),
    )
    out_specs = (P("dp", "seq", None), P(("dp", "seq"), None))
    return jax.shard_map(
        on_device, mesh=mesh, in_specs=in_specs, out_specs=out_specs, check_vma=False
    )
```

```python
import functools

import jax
import jax.numpy as jnp
from jax import lax
from jax.experimental import pallas as pl
from jax.experimental.pallas import tpu as pltpu
from jax.sharding import PartitionSpec as P

F32 = jnp.float32
BF16 = jnp.bfloat16
EPS = 1e-06
TOKENS = 128
EARLY = 32
LATE = 96
E = 1536
H = 768
Q = 384
WIDTH = 2048
HID = 256
SEMS = 200


def kernel(
    x_hbm, g1_ref, b1_ref, gu_hbm, dn_hbm, ls_ref, g2_ref, b2_ref, dh_hbm, pw_ref,
    hg_ref, gw_ref,
    xs, xl, ns, nl, guo, dno, gux, dnx, hl, ep, re, es, ex, lp, rl, wu, w, dh, dho, dht, pred,
    gp, gpall, ga, gb, ra, rb, sa, sb, ra2, rb2, s3, r3, res, fin,
    ssem, rsem, lsem,
):
    dp, seq = lax.axis_index("dp"), lax.axis_index("seq")
    x, yh, c = dp // 4, (dp // 2) % 2, dp % 2
    yl, z = seq // 8, seq % 8
    y = yh * 2 + yl

    def dev(xx, yy, zz, cc):
        return ((xx * 2 + yy // 2) * 2 + cc, (yy % 2) * 8 + zz)

    xp, xm, x2 = (x + 1) % 4, (x + 3) % 4, (x + 2) % 4
    yp, ym, y2 = (y + 1) % 4, (y + 3) % 4, (y + 2) % 4
    d_xp, d_xm = dev(xp, y, z, c), dev(xm, y, z, c)
    d_yp, d_ym = dev(x, yp, z, c), dev(x, ym, z, c)
    d_z = [None] + [dev(x, y, (z + k) % 8, c) for k in range(1, 8)]
    d_co = dev(x, y, z, 1 - c)
    d_pair = dev(x, yh * 2 + 1 - yl, z, c)

    barrier = pltpu.get_barrier_semaphore()
    peers = [d_xp, d_xm, d_yp, d_ym, d_co] + d_z[1:]
    for peer in peers:
        pl.semaphore_signal(barrier, inc=1, device_id=peer, device_id_type=pl.DeviceIdType.MESH)
    count = [0]
    sent = []

    def send(src, dst, device):
        k = count[0]
        count[0] += 1
        copy = pltpu.make_async_remote_copy(
            src_ref=src, dst_ref=dst, send_sem=ssem.at[k], recv_sem=rsem.at[k],
            device_id=device, device_id_type=pl.DeviceIdType.MESH,
        )
        copy.start()
        sent.append(copy)
        return copy

    def local(k, src, dst):
        copy = pltpu.make_async_copy(src, dst, lsem.at[k])
        copy.start()
        return copy

    c_xs = local(0, x_hbm.at[:, pl.ds(0, EARLY), :], xs)
    c_gu = local(1, gu_hbm, guo)
    c_dn = local(2, dn_hbm, dno)
    c_xl = local(3, x_hbm.at[pl.ds(yl * 8, 8), pl.ds(EARLY, LATE), :], xl)
    c_dh = local(4, dh_hbm, dh)
    rows_w = pw_ref[...].astype(F32)
    wu[z] = jnp.concatenate([rows_w[:, :H], rows_w[:, H:]], axis=0).astype(BF16)
    gain1, bias1 = g1_ref[...].reshape(1, E), b1_ref[...].reshape(1, E)

    def norm(v):
        v = v.astype(F32)
        v = v - jnp.mean(v, axis=-1, keepdims=True)
        var = jnp.mean(v * v, axis=-1, keepdims=True)
        return (v * lax.rsqrt(var + EPS) * gain1 + bias1).astype(BF16)

    def swish(values, weights):
        gate = jnp.dot(values, weights[0], preferred_element_type=F32)
        up = jnp.dot(values, weights[1], preferred_element_type=F32)
        return (gate * jax.nn.sigmoid(gate) * up).astype(BF16)

    def chunks(j):
        return (z + 4 - j) % 8, (z + 4 + j) % 8 if not isinstance(j, int) or j else z

    def norm_early(j):
        for chunk in chunks(j):
            ns[chunk, pl.ds(0, EARLY), :] = norm(xs[yl * 8 + chunk])
            ns[chunk, pl.ds(EARLY, EARLY), :] = norm(xs[(1 - yl) * 8 + chunk])

    c_xs.wait()
    norm_early(0)
    pl.semaphore_wait(barrier, len(peers))

    def piece(refs, side, core, k):
        if k < 4:
            return refs[0].at[:, pl.ds(pl.multiple_of((2 * side + core) * 384 + k * 96, 96), 96), :]
        return refs[1].at[pl.ds(pl.multiple_of((2 * side + core) * 64 + (k - 4) * 32, 32), 32), :]

    fetched, forwards = {}, []

    def fetch(*ks):
        for k in ks:
            fetched[k] = [
                send(piece((gu_hbm, dn_hbm), s, c, k), piece((gux, dnx), s, c, k), d)
                for s, d in ((0, d_yp), (1, d_ym))
            ]

    def forward(*ks):
        for k in ks:
            for s, copy in enumerate(fetched[k]):
                copy.wait_recv()
                forwards.append(same(piece((gux, dnx), s, c, k), d_co))

    def same(ref, device):
        return send(ref, ref, device)

    fetch(0, 1, 2)

    def unit(k):
        return wu.at[(z + k) % 8]

    wz = [send(unit(0), unit(0), d_z[1]), send(unit(0), unit(0), d_z[7])]

    def ffn_early(j):
        ca, cb = chunks(j)
        hidden = swish(jnp.concatenate([ns[ca], ns[cb]], axis=0), guo)
        for n in range(4):
            out = jnp.dot(hidden, dno[:, pl.ds(n * Q, Q)], preferred_element_type=F32).astype(BF16)
            cols = pl.ds((n % 2) * Q, Q)
            ep[ca, n // 2, :, cols] = out[:64]
            ep[cb, n // 2, :, cols] = out[64:]


    def ring_chunk(flow, hops):
        return (z + hops) % 8 if flow == 0 else (z + 8 - hops) % 8

    def ring_begin(p, r, far):
        slot, hops = (0, 4) if far else (4, 3)
        return [
            send(p.at[ring_chunk(f, hops), f if far else 1 - f], r.at[f, slot], d_z[1 if f == 0 else 7])
            for f in range(2)
        ]

    def ring_next(copies, p, r, slot, hops, far, subs=None):
        following = []
        for f in range(2):
            copies[f].wait_recv()
            half = f if far else 1 - f
            for sub in subs or [slice(None)]:
                both = r[f, slot, sub, :].astype(F32) + p[ring_chunk(f, hops), half, sub, :].astype(F32)
                r[f, slot, sub, :] = both.astype(BF16)
                src, dst = (r.at[f, slot], r.at[f, slot + 1]) if subs is None else (
                    r.at[f, slot, sub, :], r.at[f, slot + 1, sub, :])
                following.append(send(src, dst, d_z[1 if f == 0 else 7]))
        return following

    def ring_total(p, r, rows, half):
        return (
            p[z, half, rows, :].astype(F32) + r[half, 3, rows, :].astype(F32) + r[1 - half, 6, rows, :].astype(F32)
        )

    l_subs = [pl.ds(0, 48), pl.ds(48, 48)]
    c_gu.wait()
    c_dn.wait()
    ffn_early(0)
    e_far = ring_begin(ep, re, True)
    norm_early(1)
    ffn_early(1)
    e_near = ring_begin(ep, re, False)
    fetch(3, 4)
    for copy in wz:
        copy.wait_recv()
    wz = [send(unit(7), unit(7), d_z[1]), send(unit(1), unit(1), d_z[7])]
    norm_early(2)
    ffn_early(2)
    for copy in wz:
        copy.wait_recv()
    wz = [send(unit(6), unit(6), d_z[1]), send(unit(2), unit(2), d_z[7])]
    e_far = ring_next(e_far, ep, re, 0, 3, True)
    fetch(5)
    norm_early(3)
    ffn_early(3)
    for copy in wz:
        copy.wait_recv()
    wz = [send(unit(5), unit(5), d_z[1])]

    def prepare_late(j):
        for chunk in chunks(j):
            @pl.loop(0, LATE // 32)
            def _(i):
                rows = pl.ds(pl.multiple_of(i * 32, 32), 32)
                nl[chunk, rows, :] = norm(xl[chunk, rows, :])

        ca, cb = chunks(j)
        hidden = swish(jnp.concatenate([nl[ca], nl[cb]], axis=0), guo)
        hl[ca] = hidden[:LATE]
        hl[cb] = hidden[LATE:]

    c_xl.wait()
    prepare_late(0)
    wz[0].wait_recv()
    units = wu[...].astype(F32)
    w[x, yh, c, yl, :, pl.ds(0, H)] = units[:, :8].reshape(64, H).astype(BF16)
    w[x, yh, c, yl, :, pl.ds(H, H)] = units[:, 8:].reshape(64, H).astype(BF16)
    col_a, col_b = pl.ds(0, H), pl.ds(H, H)
    a_l, a_r, b_l, b_r = (pl.ds(k * Q, Q) for k in range(4))

    def block(xx, yy, cols):
        return w.at[xx, yy // 2, c, yy % 2, :, cols]

    def column(yy, cols):
        return w.at[:, yy // 2, c, yy % 2, :, cols]

    def slab(xx, cols):
        return w.at[xx, :, c, :, :, cols]

    wa1 = [same(block(x, y, col_a), d) for d in (d_xp, d_xm)]
    e_near = ring_next(e_near, ep, re, 4, 2, False)
    forward(0)
    prepare_late(1)
    e_far = ring_next(e_far, ep, re, 1, 2, True)
    forward(1, 2)
    wa1[0].wait_recv()
    wa1r = [same(block(xm, y, a_l), d_xp)]
    wa1[1].wait_recv()
    wa1r.append(same(block(xp, y, a_r), d_xm))
    prepare_late(2)
    e_near = ring_next(e_near, ep, re, 5, 1, False)
    forward(3)
    prepare_late(3)
    e_far = ring_next(e_far, ep, re, 2, 1, True)
    for copy in wa1r:
        copy.wait_recv()
    forward(4, 5)
    wb1 = [same(block(x, y, col_b), d) for d in (d_yp, d_ym)]

    def main_a(k):
        return [same(block(k, y, col_a), d) for d in (d_yp, d_ym)]

    def relay_a(copies, k):
        copies[0].wait_recv()
        first = same(block(k, ym, a_l), d_yp)
        copies[1].wait_recv()
        return [first, same(block(k, yp, a_r), d_ym)]

    def half_slab(xx, k, cols):
        return w.at[xx, k, c, :, :, cols]

    def main_b(k):
        return [same(half_slab(x, k, col_b), d) for d in (d_xp, d_xm)]

    def relay_b(copies, k):
        copies[0].wait_recv()
        first = same(half_slab(xm, k, b_l), d_xp)
        copies[1].wait_recv()
        return [first, same(half_slab(xp, k, b_r), d_xm)]

    def done(*groups):
        for copies in groups:
            for copy in copies:
                copy.wait_recv()

    wa2 = [main_a(0)]
    c_dho = send(dh_hbm, dho, d_co)
    for copy in forwards:
        copy.wait_recv()

    def ffn_late(j):
        ca, cb = chunks(j)
        other = swish(jnp.concatenate([nl[ca], nl[cb]], axis=0), gux)
        own = jnp.concatenate([hl[ca], hl[cb]], axis=0)
        for n in range(4):
            cols = pl.ds(n * Q, Q)
            out = jnp.dot(own, dno[:, cols], preferred_element_type=F32)
            out += jnp.dot(other, dnx[:, cols], preferred_element_type=F32)
            out = out.astype(BF16)
            cols = pl.ds((n % 2) * Q, Q)
            lp[ca, n // 2, :, cols] = out[:LATE]
            lp[cb, n // 2, :, cols] = out[LATE:]

    ffn_late(0)
    l_far = ring_begin(lp, rl, True)
    ffn_late(1)
    l_near = ring_begin(lp, rl, False)
    for copy in e_near + e_far:
        copy.wait_recv()
    for d in range(2):
        es[d] = ring_total(ep, re, pl.ds(EARLY, EARLY), d).astype(BF16)
    c_ex = send(es, ex, d_pair)
    wb1[0].wait_recv()
    wb1r = [same(block(x, ym, b_l), d_yp)]
    wb1[1].wait_recv()
    wb1r.append(same(block(x, yp, b_r), d_ym))
    wa2.append(main_a(1))

    @pl.loop(2, 4)
    def _(j):
        ffn_late(j)

    l_far = ring_next(l_far, lp, rl, 0, 3, True)
    done(wb1r)
    wb2 = [main_b(0)]
    wa2.append(main_a(2))
    wa2r = [relay_a(wa2[0], 0)]
    w_co = [same(column(y, col_a), d_co), same(slab(x, col_b), d_co)]
    c_dh.wait()
    c_dho.wait_recv()

    @pl.loop(0, 4)
    def _(xx):
        for k in range(4):
            cols = pl.ds(pl.multiple_of(xx * 512 + k * 128, 128), 128)
            for t, ref in enumerate((dh, dho)):
                turned = ref[:, cols].T
                for low in range(2):
                    dht[xx, (k // 2) * 2 + low, pl.ds((k % 2) * 64, 64), pl.ds(t * 128, 128)] = (
                        turned[low * 64:(low + 1) * 64]
                    )

    l_near = ring_next(l_near, lp, rl, 4, 2, False)
    wb2.append(main_b(1))
    wa2.append(main_a(3))
    wa2r.append(relay_a(wa2[1], 1))
    l_far = ring_next(l_far, lp, rl, 1, 2, True)
    wb2r = [relay_b(wb2[0], 0)]
    wa2r.append(relay_a(wa2[2], 2))
    l_near = ring_next(l_near, lp, rl, 5, 1, False)
    wb2r.append(relay_b(wb2[1], 1))
    wa2r.append(relay_a(wa2[3], 3))
    w_co += [same(column(yy, col_a), d_co) for yy in (ym, yp)]
    w_co += [same(slab(xx, col_b), d_co) for xx in (xm, xp)]
    l_last = ring_next(l_far, lp, rl, 2, 1, True, l_subs)
    done(*wa2r, *wb2r)
    w_co += [same(column(y2, col_a), d_co), same(slab(x2, col_b), d_co)]
    done(w_co)

    @pl.loop(0, 3)
    def _(n):
        cols = pl.ds(pl.multiple_of(n * 512, 512), 512)
        acc = jnp.zeros((TOKENS, 512), F32)
        for k in range(4):
            acc += jnp.dot(
                dh[:, pl.ds(k * 512, 512)], w[k, :, :, :, :, cols].reshape(512, 512),
                preferred_element_type=F32,
            )
        pred[:, cols] = acc

    scale, gain2, bias2 = (r[...].reshape(1, E) for r in (ls_ref, g2_ref, b2_ref))

    def loss_gradient(own, branch, rows):
        v = own.astype(F32) + scale * jnp.concatenate(branch, axis=1)
        v = v - jnp.mean(v, axis=-1, keepdims=True)
        var = jnp.mean(v * v, axis=-1, keepdims=True)
        t = v * lax.rsqrt(var + EPS) * gain2 + bias2
        p = pred[rows, :]
        inv_p = lax.rsqrt(jnp.sum(p * p, axis=-1, keepdims=True) + EPS)
        inv_t = lax.rsqrt(jnp.sum(t * t, axis=-1, keepdims=True) + EPS)
        dot = jnp.sum(p * t, axis=-1, keepdims=True)
        lead = (-1.0 * E) * (inv_p * inv_t)
        grad = (lead * (t - (dot * inv_p * inv_p) * p)).astype(BF16)
        gp[0, rows, :] = grad[:, :H]
        gp[1, rows, :] = grad[:, H:]

    def swap_gradient(start, size):
        gpall[pl.ds(start, size), :] = gp[c, pl.ds(start, size), :]
        return send(gp.at[1 - c, pl.ds(start, size), :], gpall.at[pl.ds(128 + start, size), :], d_co)

    c_ex.wait_recv()

    @pl.loop(0, EARLY // 16)
    def _(i):
        rows = pl.ds(pl.multiple_of(i * 16, 16), 16)
        branch = [ring_total(ep, re, rows, d) + ex[d, rows, :].astype(F32) for d in range(2)]
        loss_gradient(xs[yl * 8 + z, rows, :], branch, rows)

    c_gp = [swap_gradient(0, EARLY)]
    for copy in l_near:
        copy.wait_recv()
    for k in range(2):
        l_last[k].wait_recv()
        l_last[k + 2].wait_recv()

        @pl.loop(3 * k, 3 * k + 3)
        def _(i):
            rows = pl.ds(pl.multiple_of(i * 16, 16), 16)
            branch = [ring_total(lp, rl, rows, d) for d in range(2)]
            loss_gradient(xl[z, rows, :], branch, pl.ds(pl.multiple_of(EARLY + i * 16, 16), 16))

        c_gp.append(swap_gradient(EARLY + 48 * k, 48))
    for copy in c_gp:
        copy.wait_recv()

    def grad_slab(xx):
        out = jnp.dot(dht[xx].reshape(512, 256), gpall[...], preferred_element_type=F32).astype(BF16)
        for half in range(2):
            ga[xx, half] = out[half * 256:(half + 1) * 256, :Q]
        for yy in range(4):
            gb[yy, xx // 2, pl.ds(pl.multiple_of((xx % 2) * 128, 128), 128), :] = (
                out[yy * 128:(yy + 1) * 128, Q:]
            )

    def first(g, r, two, plus, minus, dplus, dminus):
        return dict(
            l2=send(g.at[two, 0], r.at[0], dplus), r2=send(g.at[two, 1], r.at[3], dminus),
        )

    def second(o, g, r, plus, minus, dplus, dminus):
        o["ro"] = send(g.at[plus, 1], r.at[1], dplus)
        o["lo"] = send(g.at[minus, 0], r.at[4], dminus)

    def relay(o, g, r, plus, minus, dplus, dminus):
        o["l2"].wait_recv()
        r[0] = (r[0].astype(F32) + g[plus, 0].astype(F32)).astype(BF16)
        o["ls"] = send(r.at[0], r.at[2], dplus)
        o["r2"].wait_recv()
        r[3] = (r[3].astype(F32) + g[minus, 1].astype(F32)).astype(BF16)
        o["rs"] = send(r.at[3], r.at[5], dminus)

    def total(o, g, r, me):
        for name in ("ro", "lo", "ls", "rs"):
            o[name].wait_recv()
        left = g[me, 0].astype(F32) + r[2].astype(F32) + r[4].astype(F32)
        right = g[me, 1].astype(F32) + r[1].astype(F32) + r[5].astype(F32)
        return left, right

    on_x, on_y = (xp, xm, d_xp, d_xm), (yp, ym, d_yp, d_ym)
    grad_slab(x2)
    oa = first(ga, ra, x2, *on_x)
    grad_slab(xp)
    grad_slab(xm)
    second(oa, ga, ra, *on_x)
    grad_slab(x)
    ob = first(gb, rb, y2, *on_y)
    second(ob, gb, rb, *on_y)

    def hidden_gradient(k):
        rows = w.at[k]
        out = jnp.zeros((TOKENS, 512), F32)
        for d in range(2):
            out += lax.dot_general(
                gp[d], rows[:, :, :, :, pl.ds(d * H, H)].reshape(512, H),
                (((1,), (1,)), ((), ())), preferred_element_type=F32,
            )
        hg_ref[0, :, pl.ds(pl.multiple_of(k * 512, 512), 512)] = out.astype(BF16)

    @pl.loop(0, 2)
    def _(k):
        hidden_gradient(k)

    relay(oa, ga, ra, *on_x)
    relay(ob, gb, rb, *on_y)

    @pl.loop(2, 4)
    def _(k):
        hidden_gradient(k)

    left, right = total(oa, ga, ra, x)
    for k, half in enumerate((left, right)):
        half = half.astype(BF16)
        for q in range(4):
            sa[2 * k + q // 2, q % 2] = half[q * 64:(q + 1) * 64]
    oa2 = first(sa, ra2, y2, *on_y)
    second(oa2, sa, ra2, *on_y)
    left, right = total(ob, gb, rb, y)
    for k, half in enumerate((left, right)):
        half = half.astype(BF16)
        for q in range(4):
            sb[2 * k + q // 2, q % 2] = half[q * 64:(q + 1) * 64]
    ob2 = first(sb, rb2, x2, *on_x)
    second(ob2, sb, rb2, *on_x)
    relay(oa2, sa, ra2, *on_y)
    relay(ob2, sb, rb2, *on_x)
    for k, (o, s, r, me) in enumerate(((oa2, sa, ra2, y), (ob2, sb, rb2, x))):
        left, right = total(o, s, r, me)
        both = jnp.concatenate([left.reshape(8, 8, Q), right.reshape(8, 8, Q)], axis=1)
        s3[:, :, pl.ds(k * Q, Q)] = both.astype(BF16)
    last = [send(s3.at[(z + k) % 8], r3.at[z], d_z[k]) for k in (4, 3, 5, 2, 6, 1, 7)]
    r3[z] = s3[z]
    for copy in last:
        copy.wait_recv()
    tot = jnp.sum(r3[...].astype(F32), axis=0) * (1.0 / (16 * 2048) ** 0.5)
    res[0] = tot[:8]
    res[1] = tot[8:]
    c_fin = send(res.at[1 - c], fin, d_co)
    gw_ref[:, pl.ds(pl.multiple_of(c * H, H), H)] = res[c]
    for copy in sent[:-1]:
        copy.wait_send()
    c_fin.wait_recv()
    gw_ref[:, pl.ds(pl.multiple_of((1 - c) * H, H), H)] = fin[...]
    c_fin.wait_send()


def on_device(
    encoder_input, sublayer_norm_gain, sublayer_norm_bias, gate_up_weight, down_weight,
    branch_layer_scale, closing_norm_gain, closing_norm_bias, diffusion_hidden, projector_weight,
):
    hbm = pl.BlockSpec(memory_space=pl.ANY)
    vmem = pl.BlockSpec(memory_space=pltpu.VMEM)
    return pl.pallas_call(
        kernel,
        out_shape=(
            jax.ShapeDtypeStruct((1, TOKENS, WIDTH), BF16),
            jax.ShapeDtypeStruct((8, E), F32),
        ),
        in_specs=[hbm, vmem, vmem, hbm, hbm, vmem, vmem, vmem, hbm, vmem],
        out_specs=(vmem, vmem),
        scratch_shapes=[
            pltpu.VMEM((16, EARLY, E), BF16),
            pltpu.VMEM((8, LATE, E), BF16),
            pltpu.VMEM((8, 2 * EARLY, E), BF16),
            pltpu.VMEM((8, LATE, E), BF16),
            pltpu.VMEM((2, E, HID), BF16),
            pltpu.VMEM((HID, E), BF16),
            pltpu.VMEM((2, E, HID), BF16),
            pltpu.VMEM((HID, E), BF16),
            pltpu.VMEM((8, LATE, HID), BF16),
            pltpu.VMEM((8, 2, 2 * EARLY, H), BF16),
            pltpu.VMEM((2, 7, 2 * EARLY, H), BF16),
            pltpu.VMEM((2, EARLY, H), BF16),
            pltpu.VMEM((2, EARLY, H), BF16),
            pltpu.VMEM((8, 2, LATE, H), BF16),
            pltpu.VMEM((2, 7, LATE, H), BF16),
            pltpu.VMEM((8, 16, H), BF16),
            pltpu.VMEM((4, 2, 2, 2, 64, E), BF16),
            pltpu.VMEM((TOKENS, WIDTH), BF16),
            pltpu.VMEM((TOKENS, WIDTH), BF16),
            pltpu.VMEM((4, 4, 128, 256), BF16),
            pltpu.VMEM((TOKENS, E), F32),
            pltpu.VMEM((2, TOKENS, H), BF16),
            pltpu.VMEM((256, H), BF16),
            pltpu.VMEM((4, 2, 256, Q), BF16),
            pltpu.VMEM((4, 2, 256, Q), BF16),
            pltpu.VMEM((6, 256, Q), BF16),
            pltpu.VMEM((6, 256, Q), BF16),
            pltpu.VMEM((4, 2, 64, Q), BF16),
            pltpu.VMEM((4, 2, 64, Q), BF16),
            pltpu.VMEM((6, 64, Q), BF16),
            pltpu.VMEM((6, 64, Q), BF16),
            pltpu.VMEM((8, 16, H), BF16),
            pltpu.VMEM((8, 16, H), BF16),
            pltpu.VMEM((2, 8, H), F32),
            pltpu.VMEM((8, H), F32),
            pltpu.SemaphoreType.DMA((SEMS,)),
            pltpu.SemaphoreType.DMA((SEMS,)),
            pltpu.SemaphoreType.DMA((5,)),
        ],
        compiler_params=pltpu.CompilerParams(
            collective_id=0, has_side_effects=True, vmem_limit_bytes=56 * 1024 * 1024
        ),
    )(
        encoder_input[0].reshape(16, TOKENS, E), sublayer_norm_gain, sublayer_norm_bias, gate_up_weight, down_weight,
        branch_layer_scale, closing_norm_gain, closing_norm_bias, diffusion_hidden[0], projector_weight,
    )


def solution(mesh):
    in_specs = (
        P("dp", None, None), P(), P(), P(None, None, "seq"), P("seq", None), P(), P(), P(),
        P("dp", "seq", None), P(("dp", "seq"), None),
    )
    out_specs = (P("dp", "seq", None), P(("dp", "seq"), None))
    return jax.shard_map(
        on_device, mesh=mesh, in_specs=in_specs, out_specs=out_specs, check_vma=False
    )
```

```python
import functools

import jax
import jax.numpy as jnp
from jax import lax
from jax.experimental import pallas as pl
from jax.experimental.pallas import tpu as pltpu
from jax.sharding import PartitionSpec as P

F32 = jnp.float32
BF16 = jnp.bfloat16
EPS = 1e-06
TOKENS = 128
EARLY = 32
LATE = 96
E = 1536
H = 768
Q = 384
WIDTH = 2048
HID = 256
SEMS = 200


def kernel(
    x_hbm, g1_ref, b1_ref, gu_hbm, dn_hbm, ls_ref, g2_ref, b2_ref, dh_hbm, pw_ref,
    hg_ref, gw_ref,
    xs, xl, ns, nl, guo, dno, gux, dnx, hl, ep, re, es, ex, lp, rl, wu, w, dh, dho, dht, pred,
    gp, gpall, ga, gb, ra, rb, sa, sb, ra2, rb2, s3, r3, res, fin,
    ssem, rsem, lsem,
):
    dp, seq = lax.axis_index("dp"), lax.axis_index("seq")
    x, yh, c = dp // 4, (dp // 2) % 2, dp % 2
    yl, z = seq // 8, seq % 8
    y = yh * 2 + yl

    def dev(xx, yy, zz, cc):
        return ((xx * 2 + yy // 2) * 2 + cc, (yy % 2) * 8 + zz)

    xp, xm, x2 = (x + 1) % 4, (x + 3) % 4, (x + 2) % 4
    yp, ym, y2 = (y + 1) % 4, (y + 3) % 4, (y + 2) % 4
    d_xp, d_xm = dev(xp, y, z, c), dev(xm, y, z, c)
    d_yp, d_ym = dev(x, yp, z, c), dev(x, ym, z, c)
    d_z = [None] + [dev(x, y, (z + k) % 8, c) for k in range(1, 8)]
    d_co = dev(x, y, z, 1 - c)
    d_pair = dev(x, yh * 2 + 1 - yl, z, c)

    barrier = pltpu.get_barrier_semaphore()
    peers = [d_xp, d_xm, d_yp, d_ym, d_co] + d_z[1:]
    for peer in peers:
        pl.semaphore_signal(barrier, inc=1, device_id=peer, device_id_type=pl.DeviceIdType.MESH)
    count = [0]
    sent = []

    def send(src, dst, device):
        k = count[0]
        count[0] += 1
        copy = pltpu.make_async_remote_copy(
            src_ref=src, dst_ref=dst, send_sem=ssem.at[k], recv_sem=rsem.at[k],
            device_id=device, device_id_type=pl.DeviceIdType.MESH,
        )
        copy.start()
        sent.append(copy)
        return copy

    def local(k, src, dst):
        copy = pltpu.make_async_copy(src, dst, lsem.at[k])
        copy.start()
        return copy

    c_xs = local(0, x_hbm.at[:, pl.ds(0, EARLY), :], xs)
    c_gu = local(1, gu_hbm, guo)
    c_dn = local(2, dn_hbm, dno)
    c_xl = local(3, x_hbm.at[pl.ds(yl * 8, 8), pl.ds(EARLY, LATE), :], xl)
    c_dh = local(4, dh_hbm, dh)
    rows_w = pw_ref[...].astype(F32)
    wu[z] = jnp.concatenate([rows_w[:, :H], rows_w[:, H:]], axis=0).astype(BF16)
    gain1, bias1 = g1_ref[...].reshape(1, E), b1_ref[...].reshape(1, E)

    def norm(v):
        v = v.astype(F32)
        v = v - jnp.mean(v, axis=-1, keepdims=True)
        var = jnp.mean(v * v, axis=-1, keepdims=True)
        return (v * lax.rsqrt(var + EPS) * gain1 + bias1).astype(BF16)

    def swish(values, weights):
        gate = jnp.dot(values, weights[0], preferred_element_type=F32)
        up = jnp.dot(values, weights[1], preferred_element_type=F32)
        return (gate * jax.nn.sigmoid(gate) * up).astype(BF16)

    def chunks(j):
        return (z + 4 - j) % 8, (z + 4 + j) % 8 if not isinstance(j, int) or j else z

    def norm_early(j):
        for chunk in chunks(j):
            ns[chunk, pl.ds(0, EARLY), :] = norm(xs[yl * 8 + chunk])
            ns[chunk, pl.ds(EARLY, EARLY), :] = norm(xs[(1 - yl) * 8 + chunk])

    c_xs.wait()
    norm_early(0)
    pl.semaphore_wait(barrier, len(peers))

    def piece(refs, side, core, k):
        if k < 4:
            return refs[0].at[:, pl.ds(pl.multiple_of((2 * side + core) * 384 + k * 96, 96), 96), :]
        return refs[1].at[pl.ds(pl.multiple_of((2 * side + core) * 64 + (k - 4) * 32, 32), 32), :]

    fetched, forwards = {}, []

    def fetch(*ks):
        for k in ks:
            fetched[k] = [
                send(piece((gu_hbm, dn_hbm), s, c, k), piece((gux, dnx), s, c, k), d)
                for s, d in ((0, d_yp), (1, d_ym))
            ]

    def forward(*ks):
        for k in ks:
            for s, copy in enumerate(fetched[k]):
                copy.wait_recv()
                forwards.append(same(piece((gux, dnx), s, c, k), d_co))

    def same(ref, device):
        return send(ref, ref, device)

    fetch(0, 1, 2)

    def unit(k):
        return wu.at[(z + k) % 8]

    wz = [send(unit(0), unit(0), d_z[1]), send(unit(0), unit(0), d_z[7])]

    def ffn_early(j):
        ca, cb = chunks(j)
        hidden = swish(jnp.concatenate([ns[ca], ns[cb]], axis=0), guo)
        for n in range(4):
            out = jnp.dot(hidden, dno[:, pl.ds(n * Q, Q)], preferred_element_type=F32).astype(BF16)
            cols = pl.ds((n % 2) * Q, Q)
            ep[ca, n // 2, :, cols] = out[:64]
            ep[cb, n // 2, :, cols] = out[64:]


    def ring_chunk(flow, hops):
        return (z + hops) % 8 if flow == 0 else (z + 8 - hops) % 8

    def ring_begin(p, r, far):
        slot, hops = (0, 4) if far else (4, 3)
        return [
            send(p.at[ring_chunk(f, hops), f if far else 1 - f], r.at[f, slot], d_z[1 if f == 0 else 7])
            for f in range(2)
        ]

    def ring_next(copies, p, r, slot, hops, far, subs=None):
        following = []
        for f in range(2):
            copies[f].wait_recv()
            half = f if far else 1 - f
            for sub in subs or [slice(None)]:
                both = r[f, slot, sub, :].astype(F32) + p[ring_chunk(f, hops), half, sub, :].astype(F32)
                r[f, slot, sub, :] = both.astype(BF16)
                src, dst = (r.at[f, slot], r.at[f, slot + 1]) if subs is None else (
                    r.at[f, slot, sub, :], r.at[f, slot + 1, sub, :])
                following.append(send(src, dst, d_z[1 if f == 0 else 7]))
        return following

    def ring_total(p, r, rows, half):
        return (
            p[z, half, rows, :].astype(F32) + r[half, 3, rows, :].astype(F32) + r[1 - half, 6, rows, :].astype(F32)
        )

    l_subs = [pl.ds(0, 48), pl.ds(48, 48)]
    c_gu.wait()
    c_dn.wait()
    ffn_early(0)
    e_far = ring_begin(ep, re, True)
    norm_early(1)
    ffn_early(1)
    e_near = ring_begin(ep, re, False)
    fetch(3, 4)
    for copy in wz:
        copy.wait_recv()
    wz = [send(unit(7), unit(7), d_z[1]), send(unit(1), unit(1), d_z[7])]
    norm_early(2)
    ffn_early(2)
    for copy in wz:
        copy.wait_recv()
    wz = [send(unit(6), unit(6), d_z[1]), send(unit(2), unit(2), d_z[7])]
    e_far = ring_next(e_far, ep, re, 0, 3, True)
    fetch(5)
    norm_early(3)
    ffn_early(3)
    for copy in wz:
        copy.wait_recv()
    wz = [send(unit(5), unit(5), d_z[1])]

    def prepare_late(j):
        for chunk in chunks(j):
            @pl.loop(0, LATE // 32)
            def _(i):
                rows = pl.ds(pl.multiple_of(i * 32, 32), 32)
                nl[chunk, rows, :] = norm(xl[chunk, rows, :])

        ca, cb = chunks(j)
        hidden = swish(jnp.concatenate([nl[ca], nl[cb]], axis=0), guo)
        hl[ca] = hidden[:LATE]
        hl[cb] = hidden[LATE:]

    c_xl.wait()
    prepare_late(0)
    wz[0].wait_recv()
    units = wu[...].astype(F32)
    w[x, yh, c, yl, :, pl.ds(0, H)] = units[:, :8].reshape(64, H).astype(BF16)
    w[x, yh, c, yl, :, pl.ds(H, H)] = units[:, 8:].reshape(64, H).astype(BF16)
    col_a, col_b = pl.ds(0, H), pl.ds(H, H)
    a_l, a_r, b_l, b_r = (pl.ds(k * Q, Q) for k in range(4))

    def block(xx, yy, cols):
        return w.at[xx, yy // 2, c, yy % 2, :, cols]

    def column(yy, cols):
        return w.at[:, yy // 2, c, yy % 2, :, cols]

    def slab(xx, cols):
        return w.at[xx, :, c, :, :, cols]

    wa1 = [same(block(x, y, col_a), d) for d in (d_xp, d_xm)]
    e_near = ring_next(e_near, ep, re, 4, 2, False)
    forward(0)
    prepare_late(1)
    e_far = ring_next(e_far, ep, re, 1, 2, True)
    forward(1, 2)
    wa1[0].wait_recv()
    wa1r = [same(block(xm, y, a_l), d_xp)]
    wa1[1].wait_recv()
    wa1r.append(same(block(xp, y, a_r), d_xm))
    prepare_late(2)
    e_near = ring_next(e_near, ep, re, 5, 1, False)
    forward(3)
    prepare_late(3)
    e_far = ring_next(e_far, ep, re, 2, 1, True)
    for copy in wa1r:
        copy.wait_recv()
    forward(4, 5)
    wb1 = [same(block(x, y, col_b), d) for d in (d_yp, d_ym)]

    def main_a(k):
        return [same(block(k, y, col_a), d) for d in (d_yp, d_ym)]

    def relay_a(copies, k):
        copies[0].wait_recv()
        first = same(block(k, ym, a_l), d_yp)
        copies[1].wait_recv()
        return [first, same(block(k, yp, a_r), d_ym)]

    def half_slab(xx, k, cols):
        return w.at[xx, k, c, :, :, cols]

    def main_b(k):
        return [same(half_slab(x, k, col_b), d) for d in (d_xp, d_xm)]

    def relay_b(copies, k):
        copies[0].wait_recv()
        first = same(half_slab(xm, k, b_l), d_xp)
        copies[1].wait_recv()
        return [first, same(half_slab(xp, k, b_r), d_xm)]

    def done(*groups):
        for copies in groups:
            for copy in copies:
                copy.wait_recv()

    wa2 = [main_a(0)]
    c_dho = send(dh_hbm, dho, d_co)
    for copy in forwards:
        copy.wait_recv()

    def ffn_late(j):
        ca, cb = chunks(j)
        other = swish(jnp.concatenate([nl[ca], nl[cb]], axis=0), gux)
        own = jnp.concatenate([hl[ca], hl[cb]], axis=0)
        for n in range(4):
            cols = pl.ds(n * Q, Q)
            out = jnp.dot(own, dno[:, cols], preferred_element_type=F32)
            out += jnp.dot(other, dnx[:, cols], preferred_element_type=F32)
            out = out.astype(BF16)
            cols = pl.ds((n % 2) * Q, Q)
            lp[ca, n // 2, :, cols] = out[:LATE]
            lp[cb, n // 2, :, cols] = out[LATE:]

    ffn_late(0)
    l_far = ring_begin(lp, rl, True)
    ffn_late(1)
    l_near = ring_begin(lp, rl, False)
    for copy in e_near + e_far:
        copy.wait_recv()
    for d in range(2):
        es[d] = ring_total(ep, re, pl.ds(EARLY, EARLY), d).astype(BF16)
    c_ex = send(es, ex, d_pair)
    wb1[0].wait_recv()
    wb1r = [same(block(x, ym, b_l), d_yp)]
    wb1[1].wait_recv()
    wb1r.append(same(block(x, yp, b_r), d_ym))
    wa2.append(main_a(1))

    @pl.loop(2, 4)
    def _(j):
        ffn_late(j)

    l_far = ring_next(l_far, lp, rl, 0, 3, True)
    done(wb1r)
    wb2 = [main_b(0)]
    wa2.append(main_a(2))
    wa2r = [relay_a(wa2[0], 0)]
    w_co = [same(column(y, col_a), d_co), same(slab(x, col_b), d_co)]
    c_dh.wait()
    c_dho.wait_recv()

    @pl.loop(0, 4)
    def _(xx):
        for k in range(4):
            cols = pl.ds(pl.multiple_of(xx * 512 + k * 128, 128), 128)
            for t, ref in enumerate((dh, dho)):
                turned = ref[:, cols].T
                for low in range(2):
                    dht[xx, (k // 2) * 2 + low, pl.ds((k % 2) * 64, 64), pl.ds(t * 128, 128)] = (
                        turned[low * 64:(low + 1) * 64]
                    )

    l_near = ring_next(l_near, lp, rl, 4, 2, False)
    wb2.append(main_b(1))
    wa2.append(main_a(3))
    wa2r.append(relay_a(wa2[1], 1))
    l_far = ring_next(l_far, lp, rl, 1, 2, True)
    wb2r = [relay_b(wb2[0], 0)]
    wa2r.append(relay_a(wa2[2], 2))
    l_near = ring_next(l_near, lp, rl, 5, 1, False)
    wb2r.append(relay_b(wb2[1], 1))
    wa2r.append(relay_a(wa2[3], 3))
    w_co += [same(column(yy, col_a), d_co) for yy in (ym, yp)]
    w_co += [same(slab(xx, col_b), d_co) for xx in (xm, xp)]
    l_last = ring_next(l_far, lp, rl, 2, 1, True, l_subs)
    done(*wa2r, *wb2r)
    w_co += [same(column(y2, col_a), d_co), same(slab(x2, col_b), d_co)]
    done(w_co)

    @pl.loop(0, 3)
    def _(n):
        cols = pl.ds(pl.multiple_of(n * 512, 512), 512)
        acc = jnp.zeros((TOKENS, 512), F32)
        for k in range(4):
            acc += jnp.dot(
                dh[:, pl.ds(k * 512, 512)], w[k, :, :, :, :, cols].reshape(512, 512),
                preferred_element_type=F32,
            )
        pred[:, cols] = acc

    scale, gain2, bias2 = (r[...].reshape(1, E) for r in (ls_ref, g2_ref, b2_ref))

    def loss_gradient(own, branch, rows):
        v = own.astype(F32) + scale * jnp.concatenate(branch, axis=1)
        v = v - jnp.mean(v, axis=-1, keepdims=True)
        var = jnp.mean(v * v, axis=-1, keepdims=True)
        t = v * lax.rsqrt(var + EPS) * gain2 + bias2
        p = pred[rows, :]
        inv_p = lax.rsqrt(jnp.sum(p * p, axis=-1, keepdims=True) + EPS)
        inv_t = lax.rsqrt(jnp.sum(t * t, axis=-1, keepdims=True) + EPS)
        dot = jnp.sum(p * t, axis=-1, keepdims=True)
        lead = (-1.0 * E) * (inv_p * inv_t)
        grad = (lead * (t - (dot * inv_p * inv_p) * p)).astype(BF16)
        gp[0, rows, :] = grad[:, :H]
        gp[1, rows, :] = grad[:, H:]

    def swap_gradient(start, size):
        gpall[pl.ds(start, size), :] = gp[c, pl.ds(start, size), :]
        return send(gp.at[1 - c, pl.ds(start, size), :], gpall.at[pl.ds(128 + start, size), :], d_co)

    c_ex.wait_recv()

    @pl.loop(0, EARLY // 16)
    def _(i):
        rows = pl.ds(pl.multiple_of(i * 16, 16), 16)
        branch = [ring_total(ep, re, rows, d) + ex[d, rows, :].astype(F32) for d in range(2)]
        loss_gradient(xs[yl * 8 + z, rows, :], branch, rows)

    c_gp = [swap_gradient(0, EARLY)]
    for copy in l_near:
        copy.wait_recv()
    for k in range(2):
        l_last[k].wait_recv()
        l_last[k + 2].wait_recv()

        @pl.loop(3 * k, 3 * k + 3)
        def _(i):
            rows = pl.ds(pl.multiple_of(i * 16, 16), 16)
            branch = [ring_total(lp, rl, rows, d) for d in range(2)]
            loss_gradient(xl[z, rows, :], branch, pl.ds(pl.multiple_of(EARLY + i * 16, 16), 16))

        c_gp.append(swap_gradient(EARLY + 48 * k, 48))
    for copy in c_gp:
        copy.wait_recv()

    def grad_slab(xx):
        out = jnp.dot(dht[xx].reshape(512, 256), gpall[...], preferred_element_type=F32).astype(BF16)
        for half in range(2):
            ga[xx, half] = out[half * 256:(half + 1) * 256, :Q]
        for yy in range(4):
            gb[yy, xx // 2, pl.ds(pl.multiple_of((xx % 2) * 128, 128), 128), :] = (
                out[yy * 128:(yy + 1) * 128, Q:]
            )

    def first(g, r, two, plus, minus, dplus, dminus):
        return dict(
            l2=send(g.at[two, 0], r.at[0], dplus), r2=send(g.at[two, 1], r.at[3], dminus),
        )

    def second(o, g, r, plus, minus, dplus, dminus):
        o["ro"] = send(g.at[plus, 1], r.at[1], dplus)
        o["lo"] = send(g.at[minus, 0], r.at[4], dminus)

    def relay(o, g, r, plus, minus, dplus, dminus):
        o["l2"].wait_recv()
        r[0] = (r[0].astype(F32) + g[plus, 0].astype(F32)).astype(BF16)
        o["ls"] = send(r.at[0], r.at[2], dplus)
        o["r2"].wait_recv()
        r[3] = (r[3].astype(F32) + g[minus, 1].astype(F32)).astype(BF16)
        o["rs"] = send(r.at[3], r.at[5], dminus)

    def total(o, g, r, me):
        for name in ("ro", "lo", "ls", "rs"):
            o[name].wait_recv()
        left = g[me, 0].astype(F32) + r[2].astype(F32) + r[4].astype(F32)
        right = g[me, 1].astype(F32) + r[1].astype(F32) + r[5].astype(F32)
        return left, right

    on_x, on_y = (xp, xm, d_xp, d_xm), (yp, ym, d_yp, d_ym)
    grad_slab(x2)
    oa = first(ga, ra, x2, *on_x)
    grad_slab(xp)
    grad_slab(xm)
    grad_slab(x)
    ob = first(gb, rb, y2, *on_y)
    second(oa, ga, ra, *on_x)
    second(ob, gb, rb, *on_y)

    def hidden_gradient(k):
        rows = w.at[k]
        out = jnp.zeros((TOKENS, 512), F32)
        for d in range(2):
            out += lax.dot_general(
                gp[d], rows[:, :, :, :, pl.ds(d * H, H)].reshape(512, H),
                (((1,), (1,)), ((), ())), preferred_element_type=F32,
            )
        hg_ref[0, :, pl.ds(pl.multiple_of(k * 512, 512), 512)] = out.astype(BF16)

    @pl.loop(0, 2)
    def _(k):
        hidden_gradient(k)

    relay(oa, ga, ra, *on_x)
    relay(ob, gb, rb, *on_y)

    @pl.loop(2, 4)
    def _(k):
        hidden_gradient(k)

    left, right = total(oa, ga, ra, x)
    for k, half in enumerate((left, right)):
        half = half.astype(BF16)
        for q in range(4):
            sa[2 * k + q // 2, q % 2] = half[q * 64:(q + 1) * 64]
    oa2 = first(sa, ra2, y2, *on_y)
    second(oa2, sa, ra2, *on_y)
    left, right = total(ob, gb, rb, y)
    for k, half in enumerate((left, right)):
        half = half.astype(BF16)
        for q in range(4):
            sb[2 * k + q // 2, q % 2] = half[q * 64:(q + 1) * 64]
    ob2 = first(sb, rb2, x2, *on_x)
    second(ob2, sb, rb2, *on_x)
    relay(oa2, sa, ra2, *on_y)
    relay(ob2, sb, rb2, *on_x)
    for k, (o, s, r, me) in enumerate(((oa2, sa, ra2, y), (ob2, sb, rb2, x))):
        left, right = total(o, s, r, me)
        both = jnp.concatenate([left.reshape(8, 8, Q), right.reshape(8, 8, Q)], axis=1)
        s3[:, :, pl.ds(k * Q, Q)] = both.astype(BF16)
    last = [send(s3.at[(z + k) % 8], r3.at[z], d_z[k]) for k in (4, 3, 5, 2, 6, 1, 7)]
    r3[z] = s3[z]
    for copy in sent[:-7]:
        copy.wait_send()
    for copy in last:
        copy.wait_recv()
    tot = jnp.sum(r3[...].astype(F32), axis=0) * (1.0 / (16 * 2048) ** 0.5)
    res[0] = tot[:8]
    res[1] = tot[8:]
    c_fin = send(res.at[1 - c], fin, d_co)
    gw_ref[:, pl.ds(pl.multiple_of(c * H, H), H)] = res[c]
    for copy in last:
        copy.wait_send()
    c_fin.wait_recv()
    gw_ref[:, pl.ds(pl.multiple_of((1 - c) * H, H), H)] = fin[...]
    c_fin.wait_send()


def on_device(
    encoder_input, sublayer_norm_gain, sublayer_norm_bias, gate_up_weight, down_weight,
    branch_layer_scale, closing_norm_gain, closing_norm_bias, diffusion_hidden, projector_weight,
):
    hbm = pl.BlockSpec(memory_space=pl.ANY)
    vmem = pl.BlockSpec(memory_space=pltpu.VMEM)
    return pl.pallas_call(
        kernel,
        out_shape=(
            jax.ShapeDtypeStruct((1, TOKENS, WIDTH), BF16),
            jax.ShapeDtypeStruct((8, E), F32),
        ),
        in_specs=[hbm, vmem, vmem, hbm, hbm, vmem, vmem, vmem, hbm, vmem],
        out_specs=(vmem, vmem),
        scratch_shapes=[
            pltpu.VMEM((16, EARLY, E), BF16),
            pltpu.VMEM((8, LATE, E), BF16),
            pltpu.VMEM((8, 2 * EARLY, E), BF16),
            pltpu.VMEM((8, LATE, E), BF16),
            pltpu.VMEM((2, E, HID), BF16),
            pltpu.VMEM((HID, E), BF16),
            pltpu.VMEM((2, E, HID), BF16),
            pltpu.VMEM((HID, E), BF16),
            pltpu.VMEM((8, LATE, HID), BF16),
            pltpu.VMEM((8, 2, 2 * EARLY, H), BF16),
            pltpu.VMEM((2, 7, 2 * EARLY, H), BF16),
            pltpu.VMEM((2, EARLY, H), BF16),
            pltpu.VMEM((2, EARLY, H), BF16),
            pltpu.VMEM((8, 2, LATE, H), BF16),
            pltpu.VMEM((2, 7, LATE, H), BF16),
            pltpu.VMEM((8, 16, H), BF16),
            pltpu.VMEM((4, 2, 2, 2, 64, E), BF16),
            pltpu.VMEM((TOKENS, WIDTH), BF16),
            pltpu.VMEM((TOKENS, WIDTH), BF16),
            pltpu.VMEM((4, 4, 128, 256), BF16),
            pltpu.VMEM((TOKENS, E), F32),
            pltpu.VMEM((2, TOKENS, H), BF16),
            pltpu.VMEM((256, H), BF16),
            pltpu.VMEM((4, 2, 256, Q), BF16),
            pltpu.VMEM((4, 2, 256, Q), BF16),
            pltpu.VMEM((6, 256, Q), BF16),
            pltpu.VMEM((6, 256, Q), BF16),
            pltpu.VMEM((4, 2, 64, Q), BF16),
            pltpu.VMEM((4, 2, 64, Q), BF16),
            pltpu.VMEM((6, 64, Q), BF16),
            pltpu.VMEM((6, 64, Q), BF16),
            pltpu.VMEM((8, 16, H), BF16),
            pltpu.VMEM((8, 16, H), BF16),
            pltpu.VMEM((2, 8, H), F32),
            pltpu.VMEM((8, H), F32),
            pltpu.SemaphoreType.DMA((SEMS,)),
            pltpu.SemaphoreType.DMA((SEMS,)),
            pltpu.SemaphoreType.DMA((5,)),
        ],
        compiler_params=pltpu.CompilerParams(
            collective_id=0, has_side_effects=True, vmem_limit_bytes=56 * 1024 * 1024
        ),
    )(
        encoder_input[0].reshape(16, TOKENS, E), sublayer_norm_gain, sublayer_norm_bias, gate_up_weight, down_weight,
        branch_layer_scale, closing_norm_gain, closing_norm_bias, diffusion_hidden[0], projector_weight,
    )


def solution(mesh):
    in_specs = (
        P("dp", None, None), P(), P(), P(None, None, "seq"), P("seq", None), P(), P(), P(),
        P("dp", "seq", None), P(("dp", "seq"), None),
    )
    out_specs = (P("dp", "seq", None), P(("dp", "seq"), None))
    return jax.shard_map(
        on_device, mesh=mesh, in_specs=in_specs, out_specs=out_specs, check_vma=False
    )
```
